32 devices in a mesh: blk: 16 (over z, y, x), lag: 2 (over core).
Axes of the slice: x: 2, y: 2, z: 4, core: 2. Of those that a mesh axis runs over, the one named last changes fastest.
Arguments:
- history: bfloat16 [64, 16384], P('lag', 'blk'), may hold values from -6 to 6
- tile_blocks: bfloat16 [2048, 128, 128], P('blk'), may hold values from -0.5 to 0.5
- tile_target: int32 [2048], P('blk'), may hold values from 0 to 7
- tile_source: int32 [2048], P('blk'), may hold values from 0 to 127, as said below
- tile_offset: int32 [2048], P('blk'), may hold values from 0 to 63
- delay_bins: int32 [128], replicated, may hold values from 0 to 63
- incident: float32 [16384], P('blk'), may hold values from -6 to 6
- self_inv: float32 [128, 128, 128], P('blk'), may hold values from -0.125 to 0.125
Outputs:
- pressure: float32 [16384], P('blk')
The draws below stay inside these ranges and needn't reach their ends.
Inputs may be any that keep to these rules, and one draw needn't show every extreme that they name: `tile_source`: among the 128 tiles of one index of blk, at most 16 have a source block on any one index of blk (source blocks i * 8 to i * 8 + 7 for index i); in every draw, for every index of blk, some index of blk is the source of exactly 16 of its tiles.
All inputs are finite; a program needn't handle non-finite values.
Results may differ from the reference program's by a relative error of at most 0.0003.
Values may be sent and summed in bfloat16 or wider, within the bound.
No kernel may reach another device: no remote copies, remote signals or barrier semaphores. Data moves between devices by JAX's collectives and lax.ppermute only.
A program may use at most 64 MiB of HBM per device.

```python
import math
import jax
import jax.numpy as jnp
import numpy as np
from jax import lax

BS = 128
NB_DEV = 8
TILE_DEV = 128
P_SIZE = 16384
NBLK = 128
L = 64
NT = 2048
CAP = 16


def draw_tile_source(key, part):
    key = jax.random.fold_in(key, 11)
    devices = NBLK // NB_DEV
    slots = devices * CAP

    def one_device(index):
        sub = jax.random.fold_in(key, index)
        key_order, key_shuffle, key_within = jax.random.split(sub, 3)
        order = jax.random.permutation(key_order, slots).astype(jnp.int32)
        favored = order[0] // CAP
        position = jnp.zeros((slots,), jnp.int32).at[order].set(jnp.arange(slots, dtype=jnp.int32))
        slot_ids = jnp.arange(slots, dtype=jnp.int32)
        score = jnp.where(slot_ids // CAP == favored, position - slots, position)
        chosen = jnp.argsort(score, stable=True)[:TILE_DEV].astype(jnp.int32)
        chosen = jax.random.permutation(key_shuffle, chosen).astype(jnp.int32)
        offsets = jax.random.randint(key_within, (TILE_DEV,), 0, NB_DEV, dtype=jnp.int32)
        return chosen // CAP * NB_DEV + offsets
    return jax.vmap(one_device)(jnp.arange(devices, dtype=jnp.int32)).reshape(NT).astype(jnp.int32)


def plant(values, rng, least, largest):
    longest = values.shape.index(max(values.shape))
    spots = []
    for shift in (0, 1):
        where = [jax.random.randint(jax.random.fold_in(rng, axis), (), 0, length) for axis, length in enumerate(values.shape)]
        where[longest] = (where[longest] + shift) % values.shape[longest]
        spots.append(tuple(where))
    return values.at[spots[0]].set(least).at[spots[1]].set(largest)


def levels(own_key, dims, shards, low, high):
    factor_of = 1.0
    for dim, shards_of in shards:
        steps = jax.random.uniform(jax.random.fold_in(jax.random.fold_in(own_key, 6), dim), (shards_of,), jnp.float32, low / len(shards), high / len(shards))
        factor_of = factor_of * jnp.repeat(jnp.exp(steps), dims[dim] // shards_of).reshape((-1,) + (1,) * (len(dims) - 1 - dim))
    return factor_of


def rank_table(number_of, slope):
    weights = [(1 << 20) // math.isqrt(rank ** slope) + 1 for rank in range(1, number_of + 1)]
    spread = 1 + sum(weights) // (1 << 30)
    return np.cumsum(np.array([max(1, weight // spread) for weight in weights]))


def skewed_ids(rng, shape, count, skew):
    table = rank_table(count, skew)
    lot = jax.random.randint(jax.random.fold_in(rng, 1), shape, 0, int(table[count - 1]))
    standing = jnp.searchsorted(jnp.asarray(table, jnp.int32), lot, side="right")
    return jax.random.permutation(jax.random.fold_in(rng, 2), count)[standing].astype(jnp.int32)


def scatter_about(rng, extent, width, reach, pieces=(), held_as=jnp.bfloat16):
    drawn = jax.random.normal(rng, extent, jnp.float32) * width
    if len(pieces) > 0:
        drawn = levels(rng, extent, pieces, -0.22, 0.18) * drawn
    return jnp.clip(drawn, min=-reach, max=reach).astype(held_as)


def setup_inputs(seed: int = 0) -> dict:
    key_list = jax.random.split(jax.random.key(seed), 9)
    return {
        "history": scatter_about(key_list[0], (L, P_SIZE), 1.0, 6.0, ((0, 2), (1, 16))),
        "tile_blocks": scatter_about(key_list[1], (NT, BS, BS), BS ** -0.5, 0.5, ((0, 16),)),
        "tile_target": plant(jax.random.randint(key_list[2], (NT,), 0, NB_DEV), jax.random.fold_in(key_list[2], 1), 0, NB_DEV - 1).astype(jnp.int32),
        "tile_source": draw_tile_source(jax.random.fold_in(key_list[8], 71), 0),
        "tile_offset": plant(skewed_ids(key_list[4], (NT,), L, 2), jax.random.fold_in(key_list[4], 3), 0, L - 1).astype(jnp.int32),
        "delay_bins": plant(jax.random.randint(key_list[5], (NBLK,), 0, L), jax.random.fold_in(key_list[5], 1), 0, L - 1).astype(jnp.int32),
        "incident": scatter_about(key_list[6], (P_SIZE,), 1.0, 6.0, ((0, 16),), jnp.float32),
        "self_inv": scatter_about(key_list[7], (NBLK, BS, BS), (BS * TILE_DEV // NB_DEV) ** -0.5, 0.125, ((0, 16),), jnp.float32),
    }


def reference(history, tile_blocks, tile_target, tile_source, tile_offset, delay_bins, incident, self_inv):
    lag_all = (tile_offset + delay_bins[tile_source]) % L
    within = jnp.arange(BS, dtype=jnp.int32)
    col_pick = (tile_source * BS)[:, None] + within[None, :]
    source_vec = history[lag_all[:, None], col_pick]
    contrib = jnp.einsum("tij,tj->ti", tile_blocks.astype(jnp.float32), source_vec.astype(jnp.float32), precision=lax.Precision.HIGHEST)
    owner_slab = (jnp.arange(NT, dtype=jnp.int32) // TILE_DEV) * NB_DEV
    global_target = owner_slab + tile_target
    summed = jax.ops.segment_sum(contrib, global_target, num_segments=NBLK)
    excite = incident.reshape(NBLK, BS) - summed
    solved = jnp.einsum("bij,bj->bi", self_inv, excite, precision=lax.Precision.HIGHEST)
    return solved.reshape(P_SIZE)
```

```python
import functools

import jax
import jax.numpy as jnp
from jax import lax
from jax.experimental import pallas as pl
from jax.experimental.pallas import tpu as pltpu
from jax.sharding import PartitionSpec as P

NT_DIMS = (((1,), (1,)), ((), ()))
VMEM = pl.BlockSpec(memory_space=pltpu.VMEM)
SMEM = pl.BlockSpec(memory_space=pltpu.SMEM)


def select_kernel(size, rows_ref, table_ref, out_ref):
    pieces, lags, width = table_ref.shape
    table = jnp.concatenate(
        [
            table_ref[p, :, b * size : (b + 1) * size]
            for p in range(pieces)
            for b in range(width // size)
        ],
        axis=0,
    )
    tiles = rows_ref.shape[1]
    lane = lax.broadcasted_iota(jnp.int32, (tiles, size), 1)
    for d in range(rows_ref.shape[0]):
        row = jnp.transpose(jnp.broadcast_to(rows_ref[d : d + 1, :], (size, tiles)))
        onehot = jnp.concatenate(
            [
                jnp.where(row == lane + first, 1.0, 0.0).astype(jnp.bfloat16)
                for first in range(0, table.shape[0], size)
            ],
            axis=1,
        )
        picked = jnp.dot(onehot, table, preferred_element_type=jnp.float32)
        out_ref[d] = picked.astype(out_ref.dtype)


def couple_kernel(target_ref, mine_ref, other_ref, tiles_ref, incident_ref, inverse_ref, out_ref):
    blocks, size = incident_ref.shape
    tiles = tiles_ref.shape[0]
    vectors = mine_ref[...].astype(jnp.float32) + other_ref[...].astype(jnp.float32)
    block_id = lax.broadcasted_iota(jnp.int32, (blocks, size), 0)
    total = jnp.zeros((blocks, size), jnp.float32)
    group = 16
    for first in range(0, tiles, group):
        left = jnp.concatenate(
            [
                jnp.where(
                    block_id == target_ref[t],
                    jnp.broadcast_to(vectors[t : t + 1, :], (blocks, size)),
                    0.0,
                ).astype(jnp.bfloat16)
                for t in range(first, first + group)
            ],
            axis=1,
        )
        right = jnp.concatenate([tiles_ref[t] for t in range(first, first + group)], axis=1)
        total = total + lax.dot_general(left, right, NT_DIMS, preferred_element_type=jnp.float32)
    excite = incident_ref[...] - total
    for b in range(blocks):
        out_ref[b : b + 1, :] = lax.dot_general(
            excite[b : b + 1, :],
            inverse_ref[b],
            NT_DIMS,
            precision=lax.Precision.HIGHEST,
            preferred_element_type=jnp.float32,
        )


def body(
    history, tile_blocks, tile_target, tile_source, tile_offset, delay_bins, incident, self_inv
):
    lag_rows = history.shape[0]
    tile_count, size = tile_blocks.shape[:2]
    slab_blocks = self_inv.shape[0]
    n_blk, n_lag = lax.axis_size("blk"), lax.axis_size("lag")
    blk, lag = lax.axis_index("blk"), lax.axis_index("lag")
    total_lags = lag_rows * n_lag
    all_blocks = delay_bins.shape[0]
    bits = n_blk.bit_length() - 1
    gather_bits = [1 << i for i in range(bits // 2)]
    exchange_bits = [1 << i for i in range(bits // 2, bits)]
    crossed = n_lag == 2

    def hop(value, bit):
        flip = 1 if crossed else 0
        pairs = [
            (j * n_lag + c, (j ^ bit) * n_lag + (c ^ flip)) for j in range(n_blk) for c in range(n_lag)
        ]
        return lax.ppermute(value, ("blk", "lag"), pairs)

    pieces = history[None]
    for bit in gather_bits:
        pieces = jnp.concatenate([pieces, hop(pieces, bit)], axis=0)
    n_pieces = pieces.shape[0]

    block_ids = jnp.arange(all_blocks, dtype=jnp.int32)
    looked = jnp.sum(
        jnp.where(tile_source[:, None] == block_ids[None, :], delay_bins[None, :], 0), axis=1
    )
    requests = (((tile_offset + looked) % total_lags) * all_blocks + tile_source)[None]
    for bit in exchange_bits:
        requests = jnp.concatenate([requests, hop(requests, bit)], axis=0)

    source = requests % all_blocks
    wanted_lag = requests // all_blocks
    piece = (source // slab_blocks) ^ blk
    if crossed:
        flips = jnp.zeros_like(piece)
        for bit in gather_bits:
            flips = flips ^ ((piece // bit) % 2)
        half = lag ^ flips
    else:
        half = lag
    lag_local = wanted_lag - half * lag_rows
    inside = (piece < n_pieces) & (lag_local >= 0) & (lag_local < lag_rows)
    row = (piece * slab_blocks + source % slab_blocks) * lag_rows + lag_local
    rows = jnp.where(inside, row, -1)

    picked = pl.pallas_call(
        functools.partial(select_kernel, size),
        out_shape=jax.ShapeDtypeStruct((rows.shape[0], tile_count, size), jnp.bfloat16),
        in_specs=[VMEM, VMEM],
        out_specs=VMEM,
        name="select",
    )(rows, pieces)

    held = picked
    for i, bit in enumerate(exchange_bits):
        held = held.reshape((-1, 2) + held.shape[1:])
        keep, send = held[:, 0], held[:, 1]
        held = keep + hop(send, bit)
    mine = held.reshape(tile_count, size)
    if n_lag == 2:
        other = lax.ppermute(mine, "lag", [(0, 1), (1, 0)])
    else:
        other = lax.psum(mine, "lag") - mine

    solved = pl.pallas_call(
        couple_kernel,
        out_shape=jax.ShapeDtypeStruct((slab_blocks, size), jnp.float32),
        in_specs=[SMEM, VMEM, VMEM, VMEM, VMEM, VMEM],
        out_specs=VMEM,
        name="couple",
    )(tile_target, mine, other, tile_blocks, incident.reshape(slab_blocks, size), self_inv)
    return solved.reshape(slab_blocks * size)


def solution(mesh):
    return jax.shard_map(
        body,
        mesh=mesh,
        in_specs=(
            P("lag", "blk"),
            P("blk", None, None),
            P("blk"),
            P("blk"),
            P("blk"),
            P(),
            P("blk"),
            P("blk", None, None),
        ),
        out_specs=P("blk"),
        check_vma=False,
    )
```

```python
import jax
import jax.numpy as jnp
from jax import lax
from jax.experimental import pallas as pl
from jax.experimental.pallas import tpu as pltpu
from jax.sharding import PartitionSpec as P

NT_DIMS = (((1,), (1,)), ((), ()))


VMEM = pl.BlockSpec(memory_space=pltpu.VMEM)
ANY = pl.BlockSpec(memory_space=pl.ANY)


def call(kernel, name, outs, held=(), loaded=(), left=(), scratch=(), cost=0):
    return pl.pallas_call(
        kernel,
        out_shape=outs,
        in_specs=[VMEM] * (len(held) + len(loaded)) + [ANY] * len(left),
        out_specs=jax.tree.map(lambda _: VMEM, outs),
        scratch_shapes=scratch,
        compiler_params=pltpu.CompilerParams(vmem_limit_bytes=16 * 1024 * 1024),
        cost_estimate=pl.CostEstimate(flops=0, bytes_accessed=cost, transcendentals=0),
        name=name,
    )(
        *(pltpu.with_memory_space_constraint(a, pltpu.VMEM) for a in held),
        *(pltpu.with_memory_space_constraint(a, pltpu.HBM) for a in loaded + left),
    )


def in_vmem(a):
    return pltpu.VMEM(a.shape, a.dtype)


def request_kernel(total_lags, shift, source_ref, offset_ref, delay_ref, history_ref, code_ref, own_ref):
    source = source_ref[...]
    lane = source.shape[1]
    chunk = 128
    looked = jnp.zeros_like(source)
    for first in range(0, delay_ref.shape[1], chunk):
        delay = jnp.transpose(jnp.broadcast_to(delay_ref[:, first : first + chunk], (lane, chunk)))
        block = lax.broadcasted_iota(jnp.int32, (chunk, lane), 0) + first
        looked = looked + jnp.sum(jnp.where(block == source, delay, 0), axis=0, keepdims=True)
    lag = offset_ref[...] + looked
    lag = jnp.where(lag >= total_lags, lag - total_lags, lag)
    code_ref[...] = (lag << shift) | source
    own_ref[...] = history_ref[...]


def join_kernel(*refs):
    pairs = len(refs) // 3
    for i in range(pairs):
        mine_ref, other_ref, out_ref = refs[2 * i], refs[2 * i + 1], refs[2 * pairs + i]
        rows = mine_ref.shape[0]
        out_ref[:rows] = mine_ref[...]
        out_ref[rows:] = other_ref[...]


def select_kernel(plan, near_ref, far_ref, *refs):
    *piece_refs, keep_ref, send_ref = refs
    size, slab_shift, shift, lag_rows, crossed = plan
    blk, lag = lax.axis_index("blk"), lax.axis_index("lag")
    slabs = [r[q] for r in piece_refs for q in range(r.shape[0])]
    width = slabs[0].shape[1]
    table = jnp.concatenate(
        [s[:, b : b + size] for s in slabs for b in range(0, width, size)], axis=0
    )
    code = jnp.concatenate([near_ref[...], far_ref[...]], axis=0)
    tiles = code.shape[1]
    source = code & ((1 << shift) - 1)
    wanted = code >> shift
    piece = (source >> slab_shift) ^ blk
    if crossed:
        flips, rest = jnp.zeros_like(piece), piece
        for _ in range((len(slabs) - 1).bit_length()):
            flips = flips ^ (rest & 1)
            rest = rest >> 1
        half = flips ^ lag
    else:
        half = jnp.zeros_like(piece) + lag
    local = wanted - half * lag_rows
    inside = (piece < len(slabs)) & (local >= 0) & (local < lag_rows)
    row = ((piece << slab_shift) + (source & ((1 << slab_shift) - 1))) * lag_rows + local
    row = jnp.where(inside, row, -1)
    lane = lax.broadcasted_iota(jnp.int32, (tiles, size), 1)
    for d in range(code.shape[0]):
        mine = jnp.transpose(jnp.broadcast_to(row[d : d + 1, :], (size, tiles)))
        onehot = jnp.concatenate(
            [
                jnp.where(mine == lane + first, 1.0, 0.0).astype(jnp.bfloat16)
                for first in range(0, table.shape[0], size)
            ],
            axis=1,
        )
        picked = jnp.dot(onehot, table, preferred_element_type=jnp.float32).astype(jnp.bfloat16)
        (send_ref if d % 2 else keep_ref)[d // 2] = picked


def stage_kernel(count, held_ref, *refs):
    sources, passed_ref, targets, sems = refs[:count], refs[count], refs[count + 1 : -1], refs[-1]
    copies = [pltpu.make_async_copy(s, t, sems.at[i]) for i, (s, t) in enumerate(zip(sources, targets))]
    for copy in copies:
        copy.start()
    passed_ref[...] = held_ref[...]
    for copy in copies:
        copy.wait()


def couple_kernel(mine_ref, other_ref, tiles_ref, target_ref, incident_ref, inverse_ref, out_ref):
    blocks, size = incident_ref.shape
    tiles = tiles_ref.shape[0]
    vectors = mine_ref[...].astype(jnp.float32) + other_ref[...].astype(jnp.float32)
    target = jnp.transpose(jnp.broadcast_to(target_ref[...], (size, tiles)))
    left = jnp.stack([jnp.where(target == b, vectors, 0.0) for b in range(blocks)], axis=0)
    left = left.astype(jnp.bfloat16).reshape(blocks, tiles * size)
    right = jnp.concatenate([tiles_ref[t] for t in range(tiles)], axis=1)
    total = lax.dot_general(left, right, NT_DIMS, preferred_element_type=jnp.float32)
    excite = incident_ref[...] - total
    lane = lax.broadcasted_iota(jnp.int32, (size, blocks), 1)
    solved = jnp.zeros((size, blocks), jnp.float32)
    for b in range(blocks):
        product = inverse_ref[b] * jnp.broadcast_to(excite[b : b + 1, :], (size, size))
        solved = jnp.where(lane == b, jnp.sum(product, axis=1, keepdims=True), solved)
    out_ref[...] = jnp.transpose(solved)


def body(
    history, tile_blocks, tile_target, tile_source, tile_offset, delay_bins, incident, self_inv
):
    lag_rows = history.shape[0]
    tile_count, size = tile_blocks.shape[:2]
    slab_blocks = self_inv.shape[0]
    n_blk, n_lag = lax.axis_size("blk"), lax.axis_size("lag")
    all_blocks = delay_bins.shape[0]
    bits = n_blk.bit_length() - 1
    shift = all_blocks.bit_length() - 1
    slab_shift = slab_blocks.bit_length() - 1
    gather_bits = [1 << i for i in range(bits // 2)]
    exchange_bits = [1 << i for i in range(bits // 2, bits)]
    crossed = n_lag == 2

    def hop(value, bit):
        flip = 1 if crossed else 0
        pairs = [
            (j * n_lag + c, (j ^ bit) * n_lag + (c ^ flip)) for j in range(n_blk) for c in range(n_lag)
        ]
        return lax.ppermute(value, ("blk", "lag"), pairs)

    first = hop(history[None], gather_bits[0])
    code, own = call(
        lambda *refs: request_kernel(lag_rows * n_lag, shift, *refs),
        "request",
        (pltpu.VMEM((1, tile_count), jnp.int32), in_vmem(history)),
        loaded=(tile_source[None], tile_offset[None], delay_bins[None], history),
    )

    pieces, arrived = own[None], first
    for i in range(max(len(exchange_bits), len(gather_bits)) - 1):
        pairs = []
        if i < len(exchange_bits) - 1:
            pairs += [code, hop(code, exchange_bits[i])]
        if i < len(gather_bits) - 1:
            pairs += [pieces, arrived]
        joined = list(
            call(
                join_kernel,
                "join",
                tuple(
                    pltpu.VMEM((2 * a.shape[0],) + a.shape[1:], a.dtype) for a in pairs[::2]
                ),
                held=tuple(pairs),
            )
        )
        if i < len(exchange_bits) - 1:
            code = joined.pop(0)
        if i < len(gather_bits) - 1:
            pieces = joined.pop(0)
            arrived = hop(pieces, gather_bits[i + 1])
    far_code, far_pieces = hop(code, exchange_bits[-1]), arrived

    half = code.shape[0]
    picked = (half, tile_count, size)
    keep, send = call(
        lambda *refs: select_kernel((size, slab_shift, shift, lag_rows, crossed), *refs),
        "select",
        (pltpu.VMEM(picked, jnp.bfloat16), pltpu.VMEM(picked, jnp.bfloat16)),
        held=(code, far_code, pieces, far_pieces),
    )

    late = (tile_blocks, tile_target[None], incident.reshape(slab_blocks, size), self_inv)
    keep, *staged = call(
        lambda *refs: stage_kernel(len(late), *refs),
        "stage",
        tuple(in_vmem(a) for a in (keep,) + late),
        held=(keep,),
        left=late,
        scratch=[pltpu.SemaphoreType.DMA((len(late),))],
        cost=tile_blocks.size * 2,
    )

    for bit in exchange_bits:
        held = keep + hop(send, bit)
        keep, send = held[0::2], held[1::2]
    mine = held.reshape(tile_count, size)
    if n_lag == 2:
        other = lax.ppermute(mine, "lag", [(0, 1), (1, 0)])
    else:
        other = lax.psum(mine, "lag") - mine

    solved = call(
        couple_kernel,
        "couple",
        jax.ShapeDtypeStruct((slab_blocks, size), jnp.float32),
        held=(mine, other) + tuple(staged),
    )
    return solved.reshape(slab_blocks * size)


def solution(mesh):
    return jax.shard_map(
        body,
        mesh=mesh,
        in_specs=(
            P("lag", "blk"),
            P("blk", None, None),
            P("blk"),
            P("blk"),
            P("blk"),
            P(),
            P("blk"),
            P("blk", None, None),
        ),
        out_specs=P("blk"),
        check_vma=False,
    )
```

```python
import jax
import jax.numpy as jnp
from jax import lax
from jax.experimental import pallas as pl
from jax.experimental.pallas import tpu as pltpu
from jax.sharding import PartitionSpec as P


VMEM = pl.BlockSpec(memory_space=pltpu.VMEM)
ANY = pl.BlockSpec(memory_space=pl.ANY)


def call(kernel, name, outs, held=(), loaded=(), left=(), scratch=(), cost=0, flops=0):
    return pl.pallas_call(
        kernel,
        out_shape=outs,
        in_specs=[VMEM] * (len(held) + len(loaded)) + [ANY] * len(left),
        out_specs=jax.tree.map(lambda _: VMEM, outs),
        scratch_shapes=scratch,
        compiler_params=pltpu.CompilerParams(vmem_limit_bytes=16 * 1024 * 1024),
        cost_estimate=pl.CostEstimate(flops=flops, bytes_accessed=cost, transcendentals=0),
        name=name,
    )(
        *(pltpu.with_memory_space_constraint(a, pltpu.VMEM) for a in held),
        *(pltpu.with_memory_space_constraint(a, pltpu.HBM) for a in loaded + left),
    )


def in_vmem(a):
    return pltpu.VMEM(a.shape, a.dtype)


def request_kernel(total_lags, shift, *refs):
    code_ref, own_ref, source_ref, offset_ref, delay_ref, sems = refs[4:]
    copies = [
        pltpu.make_async_copy(s, t, sems.at[i])
        for i, (s, t) in enumerate(zip(refs[:4], (source_ref, offset_ref, delay_ref, own_ref)))
    ]
    for copy in copies:
        copy.start()
    for copy in copies[:3]:
        copy.wait()
    source = source_ref[...]
    lane = source.shape[1]
    chunk = 128
    looked = jnp.zeros_like(source)
    for first in range(0, delay_ref.shape[1], chunk):
        delay = jnp.transpose(jnp.broadcast_to(delay_ref[:, first : first + chunk], (lane, chunk)))
        block = lax.broadcasted_iota(jnp.int32, (chunk, lane), 0) + first
        looked = looked + jnp.sum(jnp.where(block == source, delay, 0), axis=0, keepdims=True)
    lag = offset_ref[...] + looked
    lag = jnp.where(lag >= total_lags, lag - total_lags, lag)
    code_ref[...] = (lag << shift) | source
    copies[3].wait()


def join_kernel(*refs):
    pairs = len(refs) // 3
    for i in range(pairs):
        mine_ref, other_ref, out_ref = refs[2 * i], refs[2 * i + 1], refs[2 * pairs + i]
        rows = mine_ref.shape[0]
        out_ref[:rows] = mine_ref[...]
        out_ref[rows:] = other_ref[...]


def select_kernel(plan, near_ref, far_ref, *refs):
    *piece_refs, keep_ref, send_ref = refs
    size, slab_shift, shift, lag_rows, crossed = plan
    blk, lag = lax.axis_index("blk"), lax.axis_index("lag")
    slabs = [r[q] for r in piece_refs for q in range(r.shape[0])]
    width = slabs[0].shape[1]
    table = jnp.concatenate(
        [s[:, b : b + size] for s in slabs for b in range(0, width, size)], axis=0
    )
    code = jnp.concatenate([near_ref[...], far_ref[...]], axis=0)
    tiles = code.shape[1]
    source = code & ((1 << shift) - 1)
    wanted = code >> shift
    piece = (source >> slab_shift) ^ blk
    if crossed:
        flips, rest = jnp.zeros_like(piece), piece
        for _ in range((len(slabs) - 1).bit_length()):
            flips = flips ^ (rest & 1)
            rest = rest >> 1
        half = flips ^ lag
    else:
        half = jnp.zeros_like(piece) + lag
    local = wanted - half * lag_rows
    inside = (piece < len(slabs)) & (local >= 0) & (local < lag_rows)
    row = ((piece << slab_shift) + (source & ((1 << slab_shift) - 1))) * lag_rows + local
    row = jnp.where(inside, row, -1)
    lane = lax.broadcasted_iota(jnp.int32, (tiles, size), 1)
    for d in range(code.shape[0]):
        mine = jnp.transpose(jnp.broadcast_to(row[d : d + 1, :], (size, tiles)))
        onehot = jnp.concatenate(
            [
                jnp.where(mine == lane + first, 1.0, 0.0).astype(jnp.bfloat16)
                for first in range(0, table.shape[0], size)
            ],
            axis=1,
        )
        picked = jnp.dot(onehot, table, preferred_element_type=jnp.float32).astype(jnp.bfloat16)
        (send_ref if d % 2 else keep_ref)[d // 2] = picked


def stage_kernel(first, held_ref, tiles_in, *refs):
    others = (len(refs) - 4) // 2
    rest_in, passed_ref, tiles_ref = refs[:others], refs[others], refs[others + 1]
    rest_ref, buffer, sems = refs[others + 2 : -2], refs[-2], refs[-1]
    tiles, size = buffer.shape[:2]
    parts = sems.shape[0] - others
    width = tiles // parts
    copies = [
        pltpu.make_async_copy(
            tiles_in.at[pl.ds(first + i * width, width)],
            buffer.at[pl.ds(i * width, width)],
            sems.at[i],
        )
        for i in range(parts)
    ]
    rest = [
        pltpu.make_async_copy(s, t, sems.at[parts + i])
        for i, (s, t) in enumerate(zip(rest_in, rest_ref))
    ]
    for copy in copies + rest:
        copy.start()
    passed_ref[...] = held_ref[...]
    for i in range(parts):
        copies[i].wait()
        for t in range(i * width, (i + 1) * width):
            tiles_ref[t * size : (t + 1) * size, :] = jnp.transpose(buffer[t])
    for copy in rest:
        copy.wait()


def couple_kernel(mine_ref, other_ref, run0_ref, target_ref, incident_ref, run1_ref, run2_ref, inverse_ref, out_ref):
    blocks, size = incident_ref.shape
    tiles = mine_ref.shape[0]
    vectors = mine_ref[...].astype(jnp.float32) + other_ref[...].astype(jnp.float32)
    target = jnp.transpose(jnp.broadcast_to(target_ref[...], (size, tiles)))
    left = jnp.stack([jnp.where(target == b, vectors, 0.0) for b in range(blocks)], axis=0)
    left = left.astype(jnp.bfloat16).reshape(blocks, tiles * size)
    total, first = jnp.zeros((blocks, size), jnp.float32), 0
    for run_ref in (run0_ref, run1_ref, run2_ref):
        part = left[:, first : first + run_ref.shape[0]]
        total = total + jnp.dot(part, run_ref[...], preferred_element_type=jnp.float32)
        first += run_ref.shape[0]
    excite = incident_ref[...] - total
    lane = lax.broadcasted_iota(jnp.int32, (size, blocks), 1)
    solved = jnp.zeros((size, blocks), jnp.float32)
    for b in range(blocks):
        product = inverse_ref[b] * jnp.broadcast_to(excite[b : b + 1, :], (size, size))
        solved = jnp.where(lane == b, jnp.sum(product, axis=1, keepdims=True), solved)
    out_ref[...] = jnp.transpose(solved)


def body(
    history, tile_blocks, tile_target, tile_source, tile_offset, delay_bins, incident, self_inv
):
    lag_rows = history.shape[0]
    tile_count, size = tile_blocks.shape[:2]
    slab_blocks = self_inv.shape[0]
    n_blk, n_lag = lax.axis_size("blk"), lax.axis_size("lag")
    all_blocks = delay_bins.shape[0]
    bits = n_blk.bit_length() - 1
    shift = all_blocks.bit_length() - 1
    slab_shift = slab_blocks.bit_length() - 1
    gather_bits = [1 << i for i in range(bits // 2)]
    exchange_bits = [1 << i for i in range(bits // 2, bits)]
    crossed = n_lag == 2

    def hop(value, bit):
        flip = 1 if crossed else 0
        pairs = [
            (j * n_lag + c, (j ^ bit) * n_lag + (c ^ flip)) for j in range(n_blk) for c in range(n_lag)
        ]
        return lax.ppermute(value, ("blk", "lag"), pairs)

    first = hop(history[None], gather_bits[0])
    code, own = call(
        lambda *refs: request_kernel(lag_rows * n_lag, shift, *refs),
        "request",
        (pltpu.VMEM((1, tile_count), jnp.int32), in_vmem(history)),
        left=(tile_source[None], tile_offset[None], delay_bins[None], history),
        scratch=[
            pltpu.VMEM((1, tile_count), jnp.int32),
            pltpu.VMEM((1, tile_count), jnp.int32),
            pltpu.VMEM((1, all_blocks), jnp.int32),
            pltpu.SemaphoreType.DMA((4,)),
        ],
    )

    for bit in exchange_bits[:-1]:
        (code,) = call(
            join_kernel,
            "join",
            (pltpu.VMEM((2 * code.shape[0], tile_count), jnp.int32),),
            held=(code, hop(code, bit)),
            cost=1 << 28, flops=1<<35,
        )
    far_code = hop(code, exchange_bits[-1])
    pieces, arrived = own[None], first
    for bit in gather_bits[1:]:
        (pieces,) = call(
            join_kernel,
            "gather",
            (pltpu.VMEM((2 * pieces.shape[0],) + pieces.shape[1:], pieces.dtype),),
            held=(pieces, arrived),
        )
        arrived = hop(pieces, bit)
    far_pieces = arrived

    cuts = [0, tile_count // 4, tile_count * 5 // 8, tile_count]

    def stage(run, held, *rest):
        count = cuts[run + 1] - cuts[run]
        return call(
            lambda *refs: stage_kernel(cuts[run], *refs),
            "stage" + str(run),
            (in_vmem(held), pltpu.VMEM((count * size, size), tile_blocks.dtype))
            + tuple(in_vmem(a) for a in rest),
            held=(held,),
            left=(tile_blocks,) + rest,
            scratch=[
                pltpu.VMEM((count, size, size), tile_blocks.dtype),
                pltpu.SemaphoreType.DMA((max(count // 16, 1) + len(rest),)),
            ],
            cost=count * size * size * 2,
        )

    code, *staged = stage(0, code, tile_target[None], incident.reshape(slab_blocks, size))

    picked = (code.shape[0], tile_count, size)
    keep, send = call(
        lambda *refs: select_kernel((size, slab_shift, shift, lag_rows, crossed), *refs),
        "select",
        (pltpu.VMEM(picked, jnp.bfloat16), pltpu.VMEM(picked, jnp.bfloat16)),
        held=(code, far_code, pieces, far_pieces),
    )

    ended = []
    for bit in exchange_bits:
        if send.shape[0] > 1:
            passed = hop(send[1:], bit)
            ended.append(hop(send[:1], bit))
            if bit == exchange_bits[0]:
                keep, *more = stage(1, keep)
                staged += more
            send = keep[1::2] + passed[0::2]
            keep = jnp.concatenate([keep[:1], keep[2::2] + passed[1::2]], axis=0)
        else:
            keep, *more = stage(2, keep, self_inv)
            staged += more
            ended.append(hop(send, bit))
    mine = sum(ended, keep).reshape(tile_count, size)
    if n_lag == 2:
        other = lax.ppermute(mine, "lag", [(0, 1), (1, 0)])
    else:
        other = lax.psum(mine, "lag") - mine

    solved = call(
        couple_kernel,
        "couple",
        jax.ShapeDtypeStruct((slab_blocks, size), jnp.float32),
        held=(mine, other) + tuple(staged),
    )
    return solved.reshape(slab_blocks * size)


def solution(mesh):
    return jax.shard_map(
        body,
        mesh=mesh,
        in_specs=(
            P("lag", "blk"),
            P("blk", None, None),
            P("blk"),
            P("blk"),
            P("blk"),
            P(),
            P("blk"),
            P("blk", None, None),
        ),
        out_specs=P("blk"),
        check_vma=False,
    )
```

```python
import jax
import jax.numpy as jnp
from jax import lax
from jax.experimental import pallas as pl
from jax.experimental.pallas import tpu as pltpu
from jax.sharding import PartitionSpec as P


VMEM = pl.BlockSpec(memory_space=pltpu.VMEM)


def call(kernel, name, outs, *operands, weight=0):
    return pl.pallas_call(
        kernel,
        out_shape=outs,
        in_specs=[VMEM] * len(operands),
        out_specs=jax.tree.map(lambda _: VMEM, outs),
        compiler_params=pltpu.CompilerParams(vmem_limit_bytes=16 * 1024 * 1024),
        cost_estimate=pl.CostEstimate(
            flops=weight << 32, bytes_accessed=weight << 24, transcendentals=0
        ),
        name=name,
    )(*(pltpu.with_memory_space_constraint(a, pltpu.VMEM) for a in operands))


def in_vmem(a):
    return pltpu.VMEM(a.shape, a.dtype)


def ids_kernel(out_ref):
    out_ref[...] = lax.broadcasted_iota(jnp.int32, out_ref.shape, 0)


def request_kernel(total_lags, shift, ids_ref, source_ref, offset_ref, delay_ref, code_ref):
    source = source_ref[...]
    chunk, lane = ids_ref.shape
    looked = jnp.zeros_like(source)
    for first in range(0, delay_ref.shape[1], chunk):
        delay = jnp.transpose(jnp.broadcast_to(delay_ref[:, first : first + chunk], (lane, chunk)))
        block = ids_ref[...] + first
        looked = looked + jnp.sum(jnp.where(block == source, delay, 0), axis=0, keepdims=True)
    lag = offset_ref[...] + looked
    lag = jnp.where(lag >= total_lags, lag - total_lags, lag)
    code_ref[...] = (lag << shift) | source


def join_kernel(mine_ref, other_ref, out_ref):
    rows = mine_ref.shape[0]
    out_ref[:rows] = mine_ref[...]
    out_ref[rows:] = other_ref[...]


def select_kernel(plan, places, near_ref, far_ref, near_pieces_ref, far_pieces_ref, *out_refs):
    size, slab_shift, shift, lag_shift, split = plan
    blk, lag = lax.axis_index("blk"), lax.axis_index("lag")
    slabs = [r[q] for r in (near_pieces_ref, far_pieces_ref) for q in range(r.shape[0])]
    width = slabs[0].shape[1]
    table = jnp.concatenate(
        [s[:, b : b + size] for s in slabs for b in range(0, width, size)], axis=0
    )
    code = jnp.concatenate([near_ref[...], far_ref[...]], axis=0)
    tiles = code.shape[1]
    source = code & ((1 << shift) - 1)
    wanted = code >> shift
    piece = (source >> slab_shift) ^ blk
    half = wanted >> lag_shift
    if split:
        low, high = split
        same, turn = half == lag, jnp.where(lag == 0, low, high)
        slab = jnp.where((piece == 0) & same, 0, -1)
        slab = jnp.where(piece == turn, jnp.where(same, 1, 2), slab)
        slab = jnp.where((piece == low + high) & jnp.logical_not(same), 3, slab)
    else:
        slab = jnp.where((piece < len(slabs)) & (half == lag), piece, -1)
    within = ((source & ((1 << slab_shift) - 1)) << lag_shift) + (wanted & ((1 << lag_shift) - 1))
    row = (slab << (slab_shift + lag_shift)) + within
    row = jnp.where(slab >= 0, row, -1)
    lane = lax.broadcasted_iota(jnp.int32, (tiles, size), 1)
    for d, out, index in places:
        mine = jnp.transpose(jnp.broadcast_to(row[d : d + 1, :], (size, tiles)))
        onehot = jnp.concatenate(
            [
                jnp.where(mine == lane + first, 1.0, 0.0).astype(jnp.bfloat16)
                for first in range(0, table.shape[0], size)
            ],
            axis=1,
        )
        picked = jnp.dot(onehot, table, preferred_element_type=jnp.float32)
        out_refs[out][index] = picked.astype(jnp.bfloat16)


def turn_kernel(held_ref, tiles_ref, passed_ref, turned_ref):
    tiles, size = tiles_ref.shape[:2]
    passed_ref[...] = held_ref[...]
    for t in range(tiles):
        turned_ref[t * size : (t + 1) * size, :] = jnp.transpose(tiles_ref[t])


def couple_kernel(
    mine_ref, other_ref, turned_ref, target_ref, incident_ref, inverse_ref, out_ref
):
    blocks, size = incident_ref.shape
    tiles = mine_ref.shape[0]
    vectors = mine_ref[...].astype(jnp.float32) + other_ref[...].astype(jnp.float32)
    target = jnp.transpose(jnp.broadcast_to(target_ref[...], (size, tiles)))
    left = jnp.stack([jnp.where(target == b, vectors, 0.0) for b in range(blocks)], axis=0)
    left = left.astype(jnp.bfloat16).reshape(blocks, tiles * size)
    total = jnp.dot(left, turned_ref[...], preferred_element_type=jnp.float32)
    excite = incident_ref[...] - total
    lane = lax.broadcasted_iota(jnp.int32, (size, blocks), 1)
    solved = jnp.zeros((size, blocks), jnp.float32)
    for b in range(blocks):
        product = inverse_ref[b] * jnp.broadcast_to(excite[b : b + 1, :], (size, size))
        solved = jnp.where(lane == b, jnp.sum(product, axis=1, keepdims=True), solved)
    out_ref[...] = jnp.transpose(solved)


def body(
    history, tile_blocks, tile_target, tile_source, tile_offset, delay_bins, incident, self_inv
):
    lag_rows = history.shape[0]
    tile_count, size = tile_blocks.shape[:2]
    slab_blocks = self_inv.shape[0]
    n_blk, n_lag = lax.axis_size("blk"), lax.axis_size("lag")
    all_blocks = delay_bins.shape[0]
    bits = n_blk.bit_length() - 1
    shift = all_blocks.bit_length() - 1
    slab_shift = slab_blocks.bit_length() - 1
    gather_bits = [1 << i for i in range(bits // 2)]
    exchange_bits = [1 << i for i in range(bits // 2, bits)]
    lag_shift = lag_rows.bit_length() - 1
    paired = n_lag == 2 and len(gather_bits) == 2

    def hop(value, bit, other=None, flip=1):
        bits_of, flip = [bit, bit if other is None else other], flip if paired else 0
        pairs = [
            (j * n_lag + c, (j ^ bits_of[c % 2]) * n_lag + (c ^ flip))
            for j in range(n_blk)
            for c in range(n_lag)
        ]
        return lax.ppermute(value, ("blk", "lag"), pairs)

    if paired:
        first = hop(history[None], *gather_bits, flip=0)
    else:
        first = hop(history[None], gather_bits[0])
    ids = call(ids_kernel, "ids", pltpu.VMEM((min(all_blocks, 128), tile_count), jnp.int32), weight=8)
    code = call(
        lambda *refs: request_kernel(lag_rows * n_lag, shift, *refs),
        "request",
        pltpu.VMEM((1, tile_count), jnp.int32),
        ids,
        tile_source[None],
        tile_offset[None],
        delay_bins[None],
    )

    def join(name, mine, other, weight):
        shape = (2 * mine.shape[0],) + mine.shape[1:]
        return call(join_kernel, name, pltpu.VMEM(shape, mine.dtype), mine, other, weight=weight)

    for bit in exchange_bits[:0:-1]:
        code = join("join", code, hop(code, bit), 8)
    far_code = hop(code, exchange_bits[0])
    pieces, arrived = history[None], first
    for bit in gather_bits[1:]:
        pieces = join("gather", pieces, arrived, 0)
        arrived = hop(pieces, bit, gather_bits[0]) if paired else hop(pieces, bit)

    half = code.shape[0]
    plan = (size, slab_shift, shift, lag_shift, gather_bits if paired else None)

    def select(name, sizes, places, weight):
        places = [
            (sum(((d >> i) & 1) << (len(exchange_bits) - 1 - i) for i in range(len(exchange_bits))), out, k)
            for d, out, k in places
        ]
        return call(
            lambda *refs: select_kernel(plan, places, *refs),
            name,
            [pltpu.VMEM((n, tile_count, size), jnp.bfloat16) for n in sizes],
            code,
            far_code,
            pieces,
            arrived,
            weight=weight,
        )

    (send,) = select("select_send", [half - 1], [(2 * k + 1, 0, k - 1) for k in range(1, half)], 16)
    direct, keep = select(
        "select_keep", [1, half], [(1, 0, 0)] + [(2 * k, 1, k) for k in range(half)], 16
    )

    ended = []
    for bit in exchange_bits:
        if keep.shape[0] > 1:
            passed = hop(send, bit)
            ended.append(hop(direct, bit))
            onward = keep[1::2] + passed[0::2]
            direct, send = onward[:1], onward[1:]
            keep = jnp.concatenate([keep[:1], keep[2::2] + passed[1::2]], axis=0)
        else:
            keep, turned = call(
                turn_kernel,
                "turn",
                (in_vmem(keep), pltpu.VMEM((tile_count * size, size), tile_blocks.dtype)),
                keep,
                tile_blocks,
                weight=4,
            )
            ended.append(hop(direct, bit))
    mine = sum(ended, keep).reshape(tile_count, size)
    if n_lag == 2:
        other = lax.ppermute(mine, "lag", [(0, 1), (1, 0)])
    else:
        other = lax.psum(mine, "lag") - mine

    solved = call(
        couple_kernel,
        "couple",
        jax.ShapeDtypeStruct((slab_blocks, size), jnp.float32),
        mine,
        other,
        turned,
        tile_target[None],
        incident.reshape(slab_blocks, size),
        self_inv,
    )
    return solved.reshape(slab_blocks * size)


def solution(mesh):
    return jax.shard_map(
        body,
        mesh=mesh,
        in_specs=(
            P("lag", "blk"),
            P("blk", None, None),
            P("blk"),
            P("blk"),
            P("blk"),
            P(),
            P("blk"),
            P("blk", None, None),
        ),
        out_specs=P("blk"),
        check_vma=False,
    )
```

```python
import typing

import jax
import jax.numpy as jnp
from jax import lax
from jax.experimental import pallas as pl
from jax.experimental.pallas import tpu as pltpu
from jax.sharding import PartitionSpec as P


VMEM = pl.BlockSpec(memory_space=pltpu.VMEM)


class Plan(typing.NamedTuple):
    size: int
    slab_shift: int
    shift: int
    lag_shift: int
    pieces: int
    cap: int
    slots: int
    split: tuple


def call(kernel, name, outs, *operands, weight=0):
    return pl.pallas_call(
        kernel,
        out_shape=outs,
        in_specs=[VMEM] * len(operands),
        out_specs=jax.tree.map(lambda _: VMEM, outs),
        compiler_params=pltpu.CompilerParams(vmem_limit_bytes=16 * 1024 * 1024),
        cost_estimate=pl.CostEstimate(
            flops=weight << 32, bytes_accessed=weight << 24, transcendentals=0
        ),
        name=name,
    )(*(pltpu.with_memory_space_constraint(a, pltpu.VMEM) for a in operands))


def in_vmem(a):
    return pltpu.VMEM(a.shape, a.dtype)


def ids_kernel(out_ref):
    out_ref[...] = lax.broadcasted_iota(jnp.int32, out_ref.shape, 0)


def request_kernel(total_lags, shift, slab_shift, ids_ref, source_ref, offset_ref, delay_ref, code_ref):
    source = source_ref[...]
    chunk, lane = ids_ref.shape
    looked = jnp.zeros_like(source)
    for first in range(0, delay_ref.shape[1], chunk):
        delay = jnp.transpose(jnp.broadcast_to(delay_ref[:, first : first + chunk], (lane, chunk)))
        block = ids_ref[...] + first
        looked = looked + jnp.sum(jnp.where(block == source, delay, 0), axis=0, keepdims=True)
    lag = offset_ref[...] + looked
    lag = jnp.where(lag >= total_lags, lag - total_lags, lag)
    code_ref[:, :lane] = (lag << shift) | source
    owner = source >> slab_shift
    other = jnp.transpose(jnp.broadcast_to(owner, (lane, lane)))
    earlier = lax.broadcasted_iota(jnp.int32, (lane, lane), 0) < lax.broadcasted_iota(
        jnp.int32, (lane, lane), 1
    )
    alike = jnp.where((other == owner) & earlier, 1, 0)
    code_ref[:, lane:] = jnp.sum(alike, axis=0, keepdims=True)


def join_kernel(mine_ref, other_ref, out_ref):
    rows = mine_ref.shape[0]
    out_ref[:rows] = mine_ref[...]
    out_ref[rows:] = other_ref[...]


def ordinal(plan, piece, lag):
    if not plan.split:
        return jnp.where(piece < plan.pieces, piece, -1)
    low, high = plan.split
    turn = jnp.where(lag == 0, low, high)
    return jnp.where(
        piece == 0, 0, jnp.where(piece == turn, 1, jnp.where(piece == low + high, 2, -1))
    )


def select_kernel(plan, groups, near_ref, far_ref, near_pieces_ref, far_pieces_ref, *out_refs):
    size, cap, lag_shift = plan.size, plan.cap, plan.lag_shift
    blk, lag = lax.axis_index("blk"), lax.axis_index("lag")
    slabs = [r[q] for r in (near_pieces_ref, far_pieces_ref) for q in range(r.shape[0])]
    width = slabs[0].shape[1]
    table = jnp.concatenate(
        [s[:, b : b + size] for s in slabs for b in range(0, width, size)], axis=0
    )
    code = jnp.concatenate([near_ref[...], far_ref[...]], axis=0)
    tiles = code.shape[1] // 2
    address, place = code[:, :tiles], code[:, tiles:]
    source = address & ((1 << plan.shift) - 1)
    wanted = address >> plan.shift
    piece = (source >> plan.slab_shift) ^ blk
    half = wanted >> lag_shift
    if plan.split:
        low, high = plan.split
        same, turn = half == lag, jnp.where(lag == 0, low, high)
        slab = jnp.where((piece == 0) & same, 0, -1)
        slab = jnp.where(piece == turn, jnp.where(same, 1, 2), slab)
        slab = jnp.where((piece == low + high) & jnp.logical_not(same), 3, slab)
    else:
        slab = jnp.where((piece < plan.pieces) & (half == lag), piece, -1)
    inner = (source & ((1 << plan.slab_shift) - 1)) << lag_shift
    row = (slab << (plan.slab_shift + lag_shift)) + inner + (wanted & ((1 << lag_shift) - 1))
    row = jnp.where(slab >= 0, row, -1)
    rank = ordinal(plan, piece, lag)
    slot = jnp.where(rank >= 0, rank * cap + place, -1)

    def picked(chosen):
        lane = lax.broadcasted_iota(jnp.int32, chosen.shape, 1)
        onehot = jnp.concatenate(
            [
                jnp.where(chosen == lane + first, 1.0, 0.0).astype(jnp.bfloat16)
                for first in range(0, table.shape[0], size)
            ],
            axis=1,
        )
        return jnp.dot(onehot, table, preferred_element_type=jnp.float32).astype(jnp.bfloat16)

    slot_id = lax.broadcasted_iota(jnp.int32, (plan.slots, tiles), 0)
    for group, out_ref in zip(groups, out_refs):
        for k, d in enumerate(group):
            if d is None:
                out_ref[...] = picked(jnp.transpose(jnp.broadcast_to(row[:1], (size, tiles))))
            else:
                there = jnp.where(slot_id == slot[d : d + 1], row[d : d + 1] + 1, 0)
                chosen = jnp.sum(there, axis=1, keepdims=True) - 1
                chosen = jnp.broadcast_to(chosen, (plan.slots, size))
                out_ref[k * plan.slots : (k + 1) * plan.slots, :] = picked(chosen)


def turn_kernel(plan, held_ref, code_ref, tiles_ref, passed_ref, turned_ref, *map_refs):
    tiles, size = tiles_ref.shape[:2]
    passed_ref[...] = held_ref[...]
    blk, lag = lax.axis_index("blk"), lax.axis_index("lag")
    source = code_ref[:, :tiles] & ((1 << plan.shift) - 1)
    place = code_ref[:, tiles:]
    apart = (source >> plan.slab_shift) ^ blk
    piece, plane = apart & (plan.pieces - 1), apart >> (plan.pieces.bit_length() - 1)
    sender = jnp.zeros_like(plane) + lag
    if plan.split:
        for i in range(len(map_refs)):
            sender = sender ^ ((plane >> i) & 1)
    rank = ordinal(plan, piece, sender)
    for i, map_ref in enumerate(map_refs):
        column = ((plane - (1 << i)) * plan.slots) + rank * plan.cap + place
        column = jnp.where((rank >= 0) & ((plane >> i) == 1), column, -1)
        column = jnp.transpose(jnp.broadcast_to(column, (size, tiles)))[:, : map_ref.shape[1]]
        lane = lax.broadcasted_iota(jnp.int32, map_ref.shape, 1)
        map_ref[...] = jnp.where(column == lane, 1.0, 0.0).astype(map_ref.dtype)
    for t in range(tiles):
        turned_ref[t * size : (t + 1) * size, :] = jnp.transpose(tiles_ref[t])


def spread_kernel(*refs):
    hops = (len(refs) - 2) // 2
    total = refs[0][...].astype(jnp.float32)
    for map_ref, rows_ref in zip(refs[1 : 1 + hops], refs[1 + hops : 1 + 2 * hops]):
        total = total + jnp.dot(
            map_ref[...], rows_ref[...], preferred_element_type=jnp.float32
        )
    refs[-1][...] = total.astype(refs[-1].dtype)


def couple_kernel(
    mine_ref, other_ref, turned_ref, target_ref, incident_ref, inverse_ref, out_ref
):
    blocks, size = incident_ref.shape
    tiles = mine_ref.shape[0]
    vectors = mine_ref[...].astype(jnp.float32) + other_ref[...].astype(jnp.float32)
    target = jnp.transpose(jnp.broadcast_to(target_ref[...], (size, tiles)))
    left = jnp.stack([jnp.where(target == b, vectors, 0.0) for b in range(blocks)], axis=0)
    left = left.astype(jnp.bfloat16).reshape(blocks, tiles * size)
    total = jnp.dot(left, turned_ref[...], preferred_element_type=jnp.float32)
    excite = incident_ref[...] - total
    lane = lax.broadcasted_iota(jnp.int32, (size, blocks), 1)
    solved = jnp.zeros((size, blocks), jnp.float32)
    for b in range(blocks):
        product = inverse_ref[b] * jnp.broadcast_to(excite[b : b + 1, :], (size, size))
        solved = jnp.where(lane == b, jnp.sum(product, axis=1, keepdims=True), solved)
    out_ref[...] = jnp.transpose(solved)


def body(
    history, tile_blocks, tile_target, tile_source, tile_offset, delay_bins, incident, self_inv
):
    lag_rows = history.shape[0]
    tile_count, size = tile_blocks.shape[:2]
    slab_blocks = self_inv.shape[0]
    n_blk, n_lag = lax.axis_size("blk"), lax.axis_size("lag")
    all_blocks = delay_bins.shape[0]
    bits = n_blk.bit_length() - 1
    shift = all_blocks.bit_length() - 1
    slab_shift = slab_blocks.bit_length() - 1
    gather_bits = [1 << i for i in range(bits // 2)]
    exchange_bits = [1 << i for i in range(bits // 2, bits)]
    lag_shift = lag_rows.bit_length() - 1
    paired = n_lag == 2 and len(gather_bits) == 2
    cap = 2 * tile_count // n_blk
    n_pieces = 1 << len(gather_bits)
    plan = Plan(
        size,
        slab_shift,
        shift,
        lag_shift,
        n_pieces,
        cap,
        (3 if paired else n_pieces) * cap,
        tuple(gather_bits) if paired else (),
    )

    def hop(value, bit, other=None, flip=1):
        bits_of, flip = [bit, bit if other is None else other], flip if paired else 0
        pairs = [
            (j * n_lag + c, (j ^ bits_of[c % 2]) * n_lag + (c ^ flip))
            for j in range(n_blk)
            for c in range(n_lag)
        ]
        return lax.ppermute(value, ("blk", "lag"), pairs)

    if paired:
        first = hop(history[None], *gather_bits, flip=0)
    else:
        first = hop(history[None], gather_bits[0])
    ids = call(ids_kernel, "ids", pltpu.VMEM((min(all_blocks, 128), tile_count), jnp.int32), weight=8)
    code = call(
        lambda *refs: request_kernel(lag_rows * n_lag, shift, slab_shift, *refs),
        "request",
        pltpu.VMEM((1, 2 * tile_count), jnp.int32),
        ids,
        tile_source[None],
        tile_offset[None],
        delay_bins[None],
    )

    def join(name, mine, other, weight):
        shape = (2 * mine.shape[0],) + mine.shape[1:]
        return call(join_kernel, name, pltpu.VMEM(shape, mine.dtype), mine, other, weight=weight)

    own_code = code
    for bit in exchange_bits[:0:-1]:
        code = join("join", code, hop(code, bit), 8)
    far_code = hop(code, exchange_bits[0])
    pieces, arrived = history[None], first
    for bit in gather_bits[1:]:
        pieces = join("gather", pieces, arrived, 0)
        arrived = hop(pieces, bit, gather_bits[0]) if paired else hop(pieces, bit)

    n_hops = len(exchange_bits)

    def select(name, groups, rows, weight):
        def request(d):
            return sum(((d >> i) & 1) << (n_hops - 1 - i) for i in range(n_hops)) or None

        return call(
            lambda *refs: select_kernel(plan, [[request(d) for d in g] for g in groups], *refs),
            name,
            [pltpu.VMEM((n, size), jnp.bfloat16) for n in rows],
            code,
            far_code,
            pieces,
            arrived,
            weight=weight,
        )

    def passes(i):
        return [d for d in range(1 << n_hops) if d >> i > 1 and (d >> i) & 1 and d % (1 << i) == 0]

    first_pass = passes(0)
    (send,) = select("select_send", [first_pass], [plan.slots * len(first_pass)], 16)
    rest = [1] + [d for d in range(2, 1 << n_hops) if d % 2 == 0]
    *picks, keep = select(
        "select_keep", [[d] for d in rest] + [[0]], [plan.slots] * len(rest) + [tile_count], 16
    )
    held = dict(zip(rest, picks))
    landed = []
    for i, bit in enumerate(exchange_bits):
        onward, rows = passes(i), plan.slots << i
        if onward:
            if i:
                send = jnp.concatenate([held[d] for d in onward], axis=0)
            passed = hop(send, bit)
        if i == n_hops - 1:
            keep, turned, *maps = call(
                lambda *refs: turn_kernel(plan, *refs),
                "turn",
                [in_vmem(keep), pltpu.VMEM((tile_count * size, size), tile_blocks.dtype)]
                + [pltpu.VMEM((tile_count, plan.slots << k), jnp.bfloat16) for k in range(n_hops)],
                keep,
                own_code,
                tile_blocks,
                weight=4,
            )
        landed.append(hop(held[1 << i], bit))
        for k, d in enumerate(onward):
            here = d ^ (1 << i)
            held[here] = jnp.concatenate([held[here], passed[k * rows : (k + 1) * rows]], axis=0)
    mine = call(spread_kernel, "spread", in_vmem(keep), keep, *maps, *landed)
    if n_lag == 2:
        other = lax.ppermute(mine, "lag", [(0, 1), (1, 0)])
    else:
        other = lax.psum(mine, "lag") - mine

    solved = call(
        couple_kernel,
        "couple",
        jax.ShapeDtypeStruct((slab_blocks, size), jnp.float32),
        mine,
        other,
        turned,
        tile_target[None],
        incident.reshape(slab_blocks, size),
        self_inv,
    )
    return solved.reshape(slab_blocks * size)


def solution(mesh):
    return jax.shard_map(
        body,
        mesh=mesh,
        in_specs=(
            P("lag", "blk"),
            P("blk", None, None),
            P("blk"),
            P("blk"),
            P("blk"),
            P(),
            P("blk"),
            P("blk", None, None),
        ),
        out_specs=P("blk"),
        check_vma=False,
    )
```

```python
import typing

import jax
import jax.numpy as jnp
from jax import lax
from jax.experimental import pallas as pl
from jax.experimental.pallas import tpu as pltpu
from jax.sharding import PartitionSpec as P


VMEM = pl.BlockSpec(memory_space=pltpu.VMEM)


class Plan(typing.NamedTuple):
    size: int
    slab_shift: int
    shift: int
    lag_shift: int
    pieces: int
    cap: int
    slots: int
    split: tuple


def call(kernel, name, outs, *operands, weight=0):
    return pl.pallas_call(
        kernel,
        out_shape=outs,
        in_specs=[VMEM] * len(operands),
        out_specs=jax.tree.map(lambda _: VMEM, outs),
        compiler_params=pltpu.CompilerParams(vmem_limit_bytes=16 * 1024 * 1024),
        cost_estimate=pl.CostEstimate(
            flops=weight << 32, bytes_accessed=weight << 24, transcendentals=0
        ),
        name=name,
    )(*(pltpu.with_memory_space_constraint(a, pltpu.VMEM) for a in operands))


def in_vmem(a):
    return pltpu.VMEM(a.shape, a.dtype)


def ids_kernel(out_ref):
    out_ref[...] = lax.broadcasted_iota(jnp.int32, out_ref.shape, 0)


def request_kernel(total_lags, shift, slab_shift, ids_ref, source_ref, offset_ref, delay_ref, code_ref):
    source = source_ref[...]
    chunk, lane = ids_ref.shape
    looked = jnp.zeros_like(source)
    for first in range(0, delay_ref.shape[1], chunk):
        delay = jnp.transpose(jnp.broadcast_to(delay_ref[:, first : first + chunk], (lane, chunk)))
        block = ids_ref[...] + first
        looked = looked + jnp.sum(jnp.where(block == source, delay, 0), axis=0, keepdims=True)
    lag = offset_ref[...] + looked
    lag = jnp.where(lag >= total_lags, lag - total_lags, lag)
    code_ref[:, :lane] = (lag << shift) | source
    owner = source >> slab_shift
    other = jnp.transpose(jnp.broadcast_to(owner, (lane, lane)))
    earlier = lax.broadcasted_iota(jnp.int32, (lane, lane), 0) < lax.broadcasted_iota(
        jnp.int32, (lane, lane), 1
    )
    alike = jnp.where((other == owner) & earlier, 1, 0)
    code_ref[:, lane:] = jnp.sum(alike, axis=0, keepdims=True)


def join_kernel(mine_ref, other_ref, out_ref):
    rows = mine_ref.shape[0]
    out_ref[:rows] = mine_ref[...]
    out_ref[rows:] = other_ref[...]


def ordinal(plan, piece, lag):
    if not plan.split:
        return jnp.where(piece < plan.pieces, piece, -1)
    low, high = plan.split
    turn = jnp.where(lag == 0, low, high)
    return jnp.where(
        piece == 0, 0, jnp.where(piece == turn, 1, jnp.where(piece == low + high, 2, -1))
    )


def select_kernel(plan, groups, near_ref, far_ref, near_pieces_ref, far_pieces_ref, *out_refs):
    size, cap, lag_shift = plan.size, plan.cap, plan.lag_shift
    blk, lag = lax.axis_index("blk"), lax.axis_index("lag")
    slabs = [r[q] for r in (near_pieces_ref, far_pieces_ref) for q in range(r.shape[0])]
    width = slabs[0].shape[1]
    table = [s[:, b : b + size] for s in slabs for b in range(0, width, size)]
    table = jnp.concatenate(
        [jnp.concatenate(table[: len(table) // 2]), jnp.concatenate(table[len(table) // 2 :])], axis=1
    )
    depth = table.shape[0]
    code = jnp.concatenate([near_ref[...], far_ref[...]], axis=0)
    tiles = code.shape[1] // 2
    address, place = code[:, :tiles], code[:, tiles:]
    source = address & ((1 << plan.shift) - 1)
    wanted = address >> plan.shift
    piece = (source >> plan.slab_shift) ^ blk
    half = wanted >> lag_shift
    if plan.split:
        low, high = plan.split
        same, turn = half == lag, jnp.where(lag == 0, low, high)
        slab = jnp.where((piece == 0) & same, 0, -1)
        slab = jnp.where(piece == turn, jnp.where(same, 1, 2), slab)
        slab = jnp.where((piece == low + high) & jnp.logical_not(same), 3, slab)
    else:
        slab = jnp.where((piece < plan.pieces) & (half == lag), piece, -1)
    inner = (source & ((1 << plan.slab_shift) - 1)) << lag_shift
    row = (slab << (plan.slab_shift + lag_shift)) + inner + (wanted & ((1 << lag_shift) - 1))
    row = jnp.where(slab >= 0, row, -1)
    rank = ordinal(plan, piece, lag)
    slot = jnp.where(rank >= 0, rank * cap + place, -1)

    def picked(chosen):
        lane = lax.broadcasted_iota(jnp.int32, chosen.shape, 1)
        low = chosen & (depth - 1)
        onehot = jnp.concatenate(
            [
                jnp.where(low == lane + first, 1.0, 0.0).astype(jnp.bfloat16)
                for first in range(0, depth, size)
            ],
            axis=1,
        )
        both = jnp.dot(onehot, table, preferred_element_type=jnp.float32)
        upper = chosen >> (depth.bit_length() - 1)
        rows = jnp.where(upper == 0, both[:, :size], jnp.where(upper == 1, both[:, size:], 0.0))
        return rows.astype(jnp.bfloat16)

    slot_id = lax.broadcasted_iota(jnp.int32, (plan.slots, tiles), 0)
    for group, out_ref in zip(groups, out_refs):
        for k, d in enumerate(group):
            if d == 0:
                out_ref[...] = picked(jnp.transpose(jnp.broadcast_to(row[:1], (size, tiles))))
            else:
                there = jnp.where(slot_id == slot[d : d + 1], row[d : d + 1] + 1, 0)
                chosen = jnp.sum(there, axis=1, keepdims=True) - 1
                chosen = jnp.broadcast_to(chosen, (plan.slots, size))
                out_ref[k * plan.slots : (k + 1) * plan.slots, :] = picked(chosen)


def turn_kernel(
    plan, held_ref, code_ref, target_ref, tiles_ref, passed_ref, turned_ref, column_ref, *map_refs
):
    tiles, size = tiles_ref.shape[:2]
    passed_ref[...] = held_ref[...]
    column_ref[...] = jnp.transpose(jnp.broadcast_to(target_ref[...], (size, tiles)))
    blk, lag = lax.axis_index("blk"), lax.axis_index("lag")
    source = code_ref[:, :tiles] & ((1 << plan.shift) - 1)
    place = code_ref[:, tiles:]
    apart = (source >> plan.slab_shift) ^ blk
    piece, high = apart & (plan.pieces - 1), apart >> (plan.pieces.bit_length() - 1)
    hops = len(map_refs)
    plane = sum(((high >> (hops - 1 - i)) & 1) << i for i in range(hops))
    sender = jnp.zeros_like(plane) + lag
    if plan.split:
        for i in range(len(map_refs)):
            sender = sender ^ ((plane >> i) & 1)
    rank = ordinal(plan, piece, sender)
    for i, map_ref in enumerate(map_refs):
        column = ((plane - (1 << i)) * plan.slots) + rank * plan.cap + place
        column = jnp.where((rank >= 0) & ((plane >> i) == 1), column, -1)
        wide = -(-map_ref.shape[1] // size) * size
        column = jnp.transpose(jnp.broadcast_to(column, (wide, tiles)))[:, : map_ref.shape[1]]
        lane = lax.broadcasted_iota(jnp.int32, map_ref.shape, 1)
        map_ref[...] = jnp.where(column == lane, 1.0, 0.0).astype(map_ref.dtype)
    for t in range(tiles):
        turned_ref[t * size : (t + 1) * size, :] = jnp.transpose(tiles_ref[t])


def couple_kernel(turned_ref, target_ref, keep_ref, *refs):
    *refs, out_ref = refs
    hops = len(refs) // 2
    vectors = keep_ref[...].astype(jnp.float32)
    for map_ref, rows_ref in zip(refs[:hops], refs[hops:]):
        vectors = vectors + jnp.dot(
            map_ref[...], rows_ref[...], preferred_element_type=jnp.float32
        )
    tiles, size = vectors.shape
    blocks = out_ref.shape[0]
    target = target_ref[...]
    left = jnp.stack([jnp.where(target == b, vectors, 0.0) for b in range(blocks)], axis=0)
    left = left.astype(jnp.bfloat16).reshape(blocks, tiles * size)
    out_ref[...] = jnp.dot(left, turned_ref[...], preferred_element_type=jnp.float32)


def solve_kernel(mine_ref, other_ref, incident_ref, inverse_ref, out_ref):
    blocks, size = incident_ref.shape
    excite = incident_ref[...] - (mine_ref[...] + other_ref[...])
    lane = lax.broadcasted_iota(jnp.int32, (size, blocks), 1)
    solved = jnp.zeros((size, blocks), jnp.float32)
    for b in range(blocks):
        product = inverse_ref[b] * jnp.broadcast_to(excite[b : b + 1, :], (size, size))
        solved = jnp.where(lane == b, jnp.sum(product, axis=1, keepdims=True), solved)
    out_ref[...] = jnp.transpose(solved)


def body(
    history, tile_blocks, tile_target, tile_source, tile_offset, delay_bins, incident, self_inv
):
    lag_rows = history.shape[0]
    tile_count, size = tile_blocks.shape[:2]
    slab_blocks = self_inv.shape[0]
    n_blk, n_lag = lax.axis_size("blk"), lax.axis_size("lag")
    all_blocks = delay_bins.shape[0]
    bits = n_blk.bit_length() - 1
    shift = all_blocks.bit_length() - 1
    slab_shift = slab_blocks.bit_length() - 1
    gather_bits = [1 << i for i in range(bits // 2)]
    exchange_bits = [1 << i for i in range(bits - 1, bits // 2 - 1, -1)]
    lag_shift = lag_rows.bit_length() - 1
    paired = n_lag == 2 and len(gather_bits) == 2
    cap = 2 * tile_count // n_blk
    n_pieces = 1 << len(gather_bits)
    plan = Plan(
        size,
        slab_shift,
        shift,
        lag_shift,
        n_pieces,
        cap,
        (3 if paired else n_pieces) * cap,
        tuple(gather_bits) if paired else (),
    )

    def hop(value, bit, other=None, flip=1):
        bits_of, flip = [bit, bit if other is None else other], flip if paired else 0
        pairs = [
            (j * n_lag + c, (j ^ bits_of[c % 2]) * n_lag + (c ^ flip))
            for j in range(n_blk)
            for c in range(n_lag)
        ]
        return lax.ppermute(value, ("blk", "lag"), pairs)

    if paired:
        first = hop(history[None], *gather_bits, flip=0)
    else:
        first = hop(history[None], gather_bits[0])
    ids = call(ids_kernel, "ids", pltpu.VMEM((min(all_blocks, 128), tile_count), jnp.int32), weight=8)
    code = call(
        lambda *refs: request_kernel(lag_rows * n_lag, shift, slab_shift, *refs),
        "request",
        pltpu.VMEM((1, 2 * tile_count), jnp.int32),
        ids,
        tile_source[None],
        tile_offset[None],
        delay_bins[None],
    )

    def join(name, mine, other, weight):
        shape = (2 * mine.shape[0],) + mine.shape[1:]
        return call(join_kernel, name, pltpu.VMEM(shape, mine.dtype), mine, other, weight=weight)

    own_code = code
    for bit in exchange_bits[:-1]:
        code = join("join", code, hop(code, bit), 8)
    far_code = hop(code, exchange_bits[-1])
    pieces, arrived = history[None], first
    for bit in gather_bits[1:]:
        pieces = join("gather", pieces, arrived, 0)
        arrived = hop(pieces, bit, gather_bits[0]) if paired else hop(pieces, bit)

    n_hops = len(exchange_bits)

    def select(name, groups, rows, weight):
        return call(
            lambda *refs: select_kernel(plan, groups, *refs),
            name,
            [pltpu.VMEM((n, size), jnp.bfloat16) for n in rows],
            code,
            far_code,
            pieces,
            arrived,
            weight=weight,
        )

    def passes(i):
        return [d for d in range(1 << n_hops) if d >> i > 1 and (d >> i) & 1 and d % (1 << i) == 0]

    first_pass = passes(0)
    (send,) = select("select_send", [first_pass], [plan.slots * len(first_pass)], 16)
    rest = [1] + [d for d in range(2, 1 << n_hops) if d % 2 == 0]
    *picks, keep = select(
        "select_keep", [[d] for d in rest] + [[0]], [plan.slots] * len(rest) + [tile_count], 16
    )
    held = dict(zip(rest, picks))
    landed = []
    for i, bit in enumerate(exchange_bits):
        onward, rows = passes(i), plan.slots << i
        if onward:
            if i:
                send = jnp.concatenate([held[d] for d in onward], axis=0)
            passed = hop(send, bit)
        if i == n_hops - 1:
            keep, turned, targets, *maps = call(
                lambda *refs: turn_kernel(plan, *refs),
                "turn",
                [
                    in_vmem(keep),
                    pltpu.VMEM((tile_count * size, size), tile_blocks.dtype),
                    pltpu.VMEM((tile_count, size), jnp.int32),
                ]
                + [pltpu.VMEM((tile_count, plan.slots << k), jnp.bfloat16) for k in range(n_hops)],
                keep,
                own_code,
                tile_target[None],
                tile_blocks,
                weight=4,
            )
        landed.append(hop(held[1 << i], bit))
        for k, d in enumerate(onward):
            here = d ^ (1 << i)
            held[here] = jnp.concatenate([held[here], passed[k * rows : (k + 1) * rows]], axis=0)
    mine = call(
        couple_kernel,
        "couple",
        pltpu.VMEM((slab_blocks, size), jnp.float32),
        turned,
        targets,
        keep,
        *maps,
        *landed,
    )
    if n_lag == 2:
        other = lax.ppermute(mine, "lag", [(0, 1), (1, 0)])
    else:
        other = lax.psum(mine, "lag") - mine
    solved = call(
        solve_kernel,
        "solve",
        jax.ShapeDtypeStruct((slab_blocks, size), jnp.float32),
        mine,
        other,
        incident.reshape(slab_blocks, size),
        self_inv,
    )
    return solved.reshape(slab_blocks * size)


def solution(mesh):
    return jax.shard_map(
        body,
        mesh=mesh,
        in_specs=(
            P("lag", "blk"),
            P("blk", None, None),
            P("blk"),
            P("blk"),
            P("blk"),
            P(),
            P("blk"),
            P("blk", None, None),
        ),
        out_specs=P("blk"),
        check_vma=False,
    )
```

```python
import typing

import jax
import jax.numpy as jnp
from jax import lax
from jax.experimental import pallas as pl
from jax.experimental.pallas import tpu as pltpu
from jax.sharding import PartitionSpec as P


VMEM = pl.BlockSpec(memory_space=pltpu.VMEM)


class Plan(typing.NamedTuple):
    size: int
    slab_shift: int
    shift: int
    lag_shift: int
    pieces: int
    cap: int
    slots: int
    split: tuple


def call(kernel, name, outs, *operands, weight=0, scratch=()):
    return pl.pallas_call(
        kernel,
        out_shape=outs,
        in_specs=[VMEM] * len(operands),
        out_specs=jax.tree.map(lambda _: VMEM, outs),
        scratch_shapes=scratch,
        compiler_params=pltpu.CompilerParams(vmem_limit_bytes=16 * 1024 * 1024),
        cost_estimate=pl.CostEstimate(
            flops=weight << 32, bytes_accessed=weight << 24, transcendentals=0
        ),
        name=name,
    )(*(pltpu.with_memory_space_constraint(a, pltpu.VMEM) for a in operands))


def in_vmem(a):
    return pltpu.VMEM(a.shape, a.dtype)


def ids_kernel(out_ref):
    out_ref[...] = lax.broadcasted_iota(jnp.int32, out_ref.shape, 0)


def request_kernel(total_lags, shift, slab_shift, ids_ref, source_ref, offset_ref, delay_ref, code_ref):
    source = source_ref[...]
    chunk, lane = ids_ref.shape
    looked = jnp.zeros_like(source)
    for first in range(0, delay_ref.shape[1], chunk):
        delay = jnp.transpose(jnp.broadcast_to(delay_ref[:, first : first + chunk], (lane, chunk)))
        block = ids_ref[...] + first
        looked = looked + jnp.sum(jnp.where(block == source, delay, 0), axis=0, keepdims=True)
    lag = offset_ref[...] + looked
    lag = jnp.where(lag >= total_lags, lag - total_lags, lag)
    code_ref[:, :lane] = (lag << shift) | source
    owner = source >> slab_shift
    other = jnp.transpose(jnp.broadcast_to(owner, (lane, lane)))
    earlier = lax.broadcasted_iota(jnp.int32, (lane, lane), 0) < lax.broadcasted_iota(
        jnp.int32, (lane, lane), 1
    )
    alike = jnp.where((other == owner) & earlier, 1, 0)
    code_ref[:, lane:] = jnp.sum(alike, axis=0, keepdims=True)


def join_kernel(mine_ref, other_ref, out_ref):
    rows = mine_ref.shape[0]
    out_ref[:rows] = mine_ref[...]
    out_ref[rows:] = other_ref[...]


def ordinal(plan, piece, lag):
    if not plan.split:
        return jnp.where(piece < plan.pieces, piece, -1)
    low, high = plan.split
    turn = jnp.where(lag == 0, low, high)
    return jnp.where(
        piece == 0, 0, jnp.where(piece == turn, 1, jnp.where(piece == low + high, 2, -1))
    )


def select_kernel(plan, groups, near_ref, far_ref, near_pieces_ref, far_pieces_ref, *out_refs):
    size, cap, lag_shift = plan.size, plan.cap, plan.lag_shift
    blk, lag = lax.axis_index("blk"), lax.axis_index("lag")
    slabs = [r[q] for r in (near_pieces_ref, far_pieces_ref) for q in range(r.shape[0])]
    width = slabs[0].shape[1]
    table = [s[:, b : b + size] for s in slabs for b in range(0, width, size)]
    table = jnp.concatenate(
        [jnp.concatenate(table[: len(table) // 2]), jnp.concatenate(table[len(table) // 2 :])], axis=1
    )
    depth = table.shape[0]
    code = jnp.concatenate([near_ref[...], far_ref[...]], axis=0)
    tiles = code.shape[1] // 2
    address, place = code[:, :tiles], code[:, tiles:]
    source = address & ((1 << plan.shift) - 1)
    wanted = address >> plan.shift
    piece = (source >> plan.slab_shift) ^ blk
    half = wanted >> lag_shift
    if plan.split:
        low, high = plan.split
        same, turn = half == lag, jnp.where(lag == 0, low, high)
        slab = jnp.where((piece == 0) & same, 0, -1)
        slab = jnp.where(piece == turn, jnp.where(same, 1, 2), slab)
        slab = jnp.where((piece == low + high) & jnp.logical_not(same), 3, slab)
    else:
        slab = jnp.where((piece < plan.pieces) & (half == lag), piece, -1)
    inner = (source & ((1 << plan.slab_shift) - 1)) << lag_shift
    row = (slab << (plan.slab_shift + lag_shift)) + inner + (wanted & ((1 << lag_shift) - 1))
    row = jnp.where(slab >= 0, row, -1)
    rank = ordinal(plan, piece, lag)
    slot = jnp.where(rank >= 0, rank * cap + place, -1)

    def picked(chosen):
        lane = lax.broadcasted_iota(jnp.int32, chosen.shape, 1)
        low = chosen & (depth - 1)
        onehot = jnp.concatenate(
            [
                jnp.where(low == lane + first, 1.0, 0.0).astype(jnp.bfloat16)
                for first in range(0, depth, size)
            ],
            axis=1,
        )
        both = jnp.dot(onehot, table, preferred_element_type=jnp.float32)
        upper = chosen >> (depth.bit_length() - 1)
        rows = jnp.where(upper == 0, both[:, :size], jnp.where(upper == 1, both[:, size:], 0.0))
        return rows.astype(jnp.bfloat16)

    slot_id = lax.broadcasted_iota(jnp.int32, (plan.slots, tiles), 0)
    for group, out_ref in zip(groups, out_refs):
        for k, d in enumerate(group):
            there = jnp.where(slot_id == slot[d : d + 1], row[d : d + 1] + 1, 0)
            chosen = jnp.sum(there, axis=1, keepdims=True) - 1
            chosen = jnp.broadcast_to(chosen, (plan.slots, size))
            out_ref[k * plan.slots : (k + 1) * plan.slots, :] = picked(chosen)


def order_kernel(
    plan, hops, count, code_ref, target_ref, held_ref, tiles_ref, passed_ref, tile_ref, column_ref, turned_ref, *scratch
):
    tiles, size = tiles_ref.shape[:2]
    passed_ref[...] = held_ref[...]
    blk, lag = lax.axis_index("blk"), lax.axis_index("lag")
    source = code_ref[:, :tiles] & ((1 << plan.shift) - 1)
    place = code_ref[:, tiles:]
    apart = (source >> plan.slab_shift) ^ blk
    piece, high = apart & (plan.pieces - 1), apart >> (plan.pieces.bit_length() - 1)
    plane = sum(((high >> (hops - 1 - i)) & 1) << i for i in range(hops))
    sender = jnp.zeros_like(plane) + lag
    if plan.split:
        for i in range(hops):
            sender = sender ^ ((plane >> i) & 1)
    rank = ordinal(plan, piece, sender)
    slot = jnp.where(rank >= 0, plane * plan.slots + rank * plan.cap + place, -1)
    wide = tile_ref.shape[1]
    slot = jnp.transpose(jnp.broadcast_to(slot, (wide, tiles)))
    target = jnp.transpose(jnp.broadcast_to(target_ref[...], (wide, tiles)))
    here = slot == lax.broadcasted_iota(jnp.int32, (tiles, wide), 1)
    tile = jnp.where(here, lax.broadcasted_iota(jnp.int32, (tiles, wide), 0), 0)
    tile_ref[...] = jnp.minimum(jnp.sum(tile, axis=0, keepdims=True), tiles - 1)
    target = jnp.sum(jnp.where(here, target + 1, 0), axis=0, keepdims=True) - 1
    column_ref[...] = jnp.transpose(jnp.broadcast_to(target, (size, wide)))[: column_ref.shape[0], :]
    turn(0, count, tile_ref, tiles_ref, turned_ref, *scratch)


def turn(first, count, tile_ref, tiles_ref, turned_ref, index, sem):
    copy = pltpu.make_async_copy(tile_ref, index, sem)
    copy.start()
    copy.wait()
    size = tiles_ref.shape[1]
    for s in range(count):
        turned_ref[s * size : (s + 1) * size, :] = jnp.transpose(tiles_ref[index[0, first + s]])


def turn_kernel(first, count, held_ref, tile_ref, tiles_ref, passed_ref, turned_ref, *scratch):
    passed_ref[...] = held_ref[...]
    turn(first, count, tile_ref, tiles_ref, turned_ref, *scratch)


def products(first, column_ref, row_refs, turned_refs, blocks):
    rows = jnp.concatenate([r[...] for r in row_refs], axis=0).astype(jnp.float32)
    count, size = rows.shape
    target = column_ref[first : first + count, :]
    left = jnp.stack([jnp.where(target == b, rows, 0.0) for b in range(blocks)], axis=0)
    left = left.astype(jnp.bfloat16)
    total = jnp.zeros((blocks, size), jnp.float32)
    for turned_ref, start, held in turned_refs:
        low, high = max(first, start), min(first + count, start + held)
        if low < high:
            part = left[:, low - first : high - first].reshape(blocks, (high - low) * size)
            total = total + jnp.dot(
                part,
                turned_ref[(low - start) * size : (high - start) * size, :],
                preferred_element_type=jnp.float32,
            )
    return total


def early_kernel(cuts, n_rows, column_ref, tile_ref, tiles_ref, turned0_ref, turned1_ref, *refs):
    row_refs, (sum_ref, turned_ref, index, sem) = refs[:n_rows], refs[n_rows:]
    turned = [(turned0_ref, cuts[0], cuts[1] - cuts[0]), (turned1_ref, cuts[1], cuts[2] - cuts[1])]
    sum_ref[...] = products(0, column_ref, row_refs, turned, sum_ref.shape[0])
    turn(cuts[2], cuts[3] - cuts[2], tile_ref, tiles_ref, turned_ref, index, sem)


def couple_kernel(cuts, early_ref, column_ref, turned1_ref, turned2_ref, rows_ref, out_ref):
    turned = [(turned1_ref, cuts[1], cuts[2] - cuts[1]), (turned2_ref, cuts[2], cuts[3] - cuts[2])]
    first = cuts[3] - rows_ref.shape[0]
    out_ref[...] = early_ref[...] + products(first, column_ref, [rows_ref], turned, out_ref.shape[0])


def solve_kernel(mine_ref, other_ref, incident_ref, inverse_ref, out_ref):
    blocks, size = incident_ref.shape
    excite = incident_ref[...] - (mine_ref[...] + other_ref[...])
    lane = lax.broadcasted_iota(jnp.int32, (size, blocks), 1)
    solved = jnp.zeros((size, blocks), jnp.float32)
    for b in range(blocks):
        product = inverse_ref[b] * jnp.broadcast_to(excite[b : b + 1, :], (size, size))
        solved = jnp.where(lane == b, jnp.sum(product, axis=1, keepdims=True), solved)
    out_ref[...] = jnp.transpose(solved)


def body(
    history, tile_blocks, tile_target, tile_source, tile_offset, delay_bins, incident, self_inv
):
    lag_rows = history.shape[0]
    tile_count, size = tile_blocks.shape[:2]
    slab_blocks = self_inv.shape[0]
    n_blk, n_lag = lax.axis_size("blk"), lax.axis_size("lag")
    all_blocks = delay_bins.shape[0]
    bits = n_blk.bit_length() - 1
    shift = all_blocks.bit_length() - 1
    slab_shift = slab_blocks.bit_length() - 1
    gather_bits = [1 << i for i in range(bits // 2)]
    exchange_bits = [1 << i for i in range(bits - 1, bits // 2 - 1, -1)]
    lag_shift = lag_rows.bit_length() - 1
    paired = n_lag == 2 and len(gather_bits) == 2
    cap = 2 * tile_count // n_blk
    n_pieces = 1 << len(gather_bits)
    plan = Plan(
        size,
        slab_shift,
        shift,
        lag_shift,
        n_pieces,
        cap,
        (3 if paired else n_pieces) * cap,
        tuple(gather_bits) if paired else (),
    )

    def hop(value, bit, other=None, flip=1):
        bits_of, flip = [bit, bit if other is None else other], flip if paired else 0
        pairs = [
            (j * n_lag + c, (j ^ bits_of[c % 2]) * n_lag + (c ^ flip))
            for j in range(n_blk)
            for c in range(n_lag)
        ]
        return lax.ppermute(value, ("blk", "lag"), pairs)

    if paired:
        first = hop(history[None], *gather_bits, flip=0)
    else:
        first = hop(history[None], gather_bits[0])
    ids = call(ids_kernel, "ids", pltpu.VMEM((min(all_blocks, 128), tile_count), jnp.int32), weight=8)
    code = call(
        lambda *refs: request_kernel(lag_rows * n_lag, shift, slab_shift, *refs),
        "request",
        pltpu.VMEM((1, 2 * tile_count), jnp.int32),
        ids,
        tile_source[None],
        tile_offset[None],
        delay_bins[None],
        weight=0,
    )

    def join(name, mine, other, weight, *extra):
        shape = (2 * mine.shape[0],) + mine.shape[1:]
        return call(
            lambda *refs: join_kernel(refs[0], refs[1], refs[-1]),
            name,
            pltpu.VMEM(shape, mine.dtype),
            mine,
            other,
            *extra,
            weight=weight,
        )

    own_code = code
    for bit in exchange_bits[:-1]:
        code = join("join", code, hop(code, bit), 8)
    far_code = hop(code, exchange_bits[-1])
    pieces, arrived = history[None], first
    for bit in gather_bits[1:]:
        pieces = join("gather", pieces, arrived, 0, tile_blocks)
        arrived = hop(pieces, bit, gather_bits[0]) if paired else hop(pieces, bit)

    n_hops = len(exchange_bits)

    n_slots = plan.slots << n_hops
    cuts = [0, n_slots // 64 * 16, n_slots // 192 * 112, n_slots]
    wide = -(-n_slots // 128) * 128
    scratch = [pltpu.SMEM((1, wide), jnp.int32), pltpu.SemaphoreType.DMA]

    def turned_tiles(run):
        return pltpu.VMEM(((cuts[run + 1] - cuts[run]) * size, size), tile_blocks.dtype)

    code, slot_tiles, columns, turned0 = call(
        lambda *refs: order_kernel(plan, n_hops, cuts[1], *refs),
        "order",
        (in_vmem(code), pltpu.VMEM((1, wide), jnp.int32), pltpu.VMEM((n_slots, size), jnp.int32), turned_tiles(0)),
        own_code,
        tile_target[None],
        code,
        tile_blocks,
        weight=0,
        scratch=scratch,
    )

    def select(name, groups, rows, weight, *after):
        return call(
            lambda *refs: select_kernel(plan, groups, *refs[len(after) :]),
            name,
            [pltpu.VMEM((n, size), jnp.bfloat16) for n in rows],
            *after,
            code,
            far_code,
            pieces,
            arrived,
            weight=weight,
        )

    def passes(i):
        return [d for d in range(1 << n_hops) if d >> i > 1 and (d >> i) & 1 and d % (1 << i) == 0]

    first_pass = passes(0) + [1]
    (send,) = select("select_send", [first_pass], [plan.slots * len(first_pass)], 16)
    rest = [d for d in range(2, 1 << n_hops) if d % 2 == 0]
    *picks, keep = select("select_keep", [[d] for d in rest + [0]], [plan.slots] * (len(rest) + 1), 16, send)
    held = dict(zip(rest, picks))
    keep, turned1 = call(
        lambda *refs: turn_kernel(cuts[1], cuts[2] - cuts[1], *refs),
        "turn",
        (in_vmem(keep), turned_tiles(1)),
        keep,
        slot_tiles,
        tile_blocks,
        weight=4,
        scratch=scratch,
    )
    landed = []
    for i, bit in enumerate(exchange_bits):
        onward, rows = passes(i), plan.slots << i
        if onward:
            if i:
                send = jnp.concatenate([held[d] for d in onward + [1 << i]], axis=0)
            passed = hop(send, bit)
            landed.append(passed[len(onward) * rows :])
        if i == n_hops - 1:
            early, turned2 = call(
                lambda *refs: early_kernel(cuts, n_hops, *refs),
                "early",
                (pltpu.VMEM((slab_blocks, size), jnp.float32), turned_tiles(2)),
                columns,
                slot_tiles,
                tile_blocks,
                turned0,
                turned1,
                keep,
                *landed,
                weight=4,
                scratch=scratch,
            )
        if not onward:
            landed.append(hop(held[1 << i], bit))
        for k, d in enumerate(onward):
            here = d ^ (1 << i)
            held[here] = jnp.concatenate([held[here], passed[k * rows : (k + 1) * rows]], axis=0)
    mine = call(
        lambda *refs: couple_kernel(cuts, *refs),
        "couple",
        pltpu.VMEM((slab_blocks, size), jnp.float32),
        early,
        columns,
        turned1,
        turned2,
        landed[-1],
    )
    if n_lag == 2:
        other = lax.ppermute(mine, "lag", [(0, 1), (1, 0)])
    else:
        other = lax.psum(mine, "lag") - mine
    solved = call(
        solve_kernel,
        "solve",
        jax.ShapeDtypeStruct((slab_blocks, size), jnp.float32),
        mine,
        other,
        incident.reshape(slab_blocks, size),
        self_inv,
    )
    return solved.reshape(slab_blocks * size)


def solution(mesh):
    return jax.shard_map(
        body,
        mesh=mesh,
        in_specs=(
            P("lag", "blk"),
            P("blk", None, None),
            P("blk"),
            P("blk"),
            P("blk"),
            P(),
            P("blk"),
            P("blk", None, None),
        ),
        out_specs=P("blk"),
        check_vma=False,
    )
```

```python
import typing

import jax
import jax.numpy as jnp
from jax import lax
from jax.experimental import pallas as pl
from jax.experimental.pallas import tpu as pltpu
from jax.sharding import PartitionSpec as P


VMEM = pl.BlockSpec(memory_space=pltpu.VMEM)


class Plan(typing.NamedTuple):
    size: int
    slab_shift: int
    shift: int
    lag_shift: int
    pieces: int
    cap: int
    slots: int
    split: tuple


def call(kernel, name, outs, *operands, weight=0, scratch=()):
    return pl.pallas_call(
        kernel,
        out_shape=outs,
        in_specs=[VMEM] * len(operands),
        out_specs=jax.tree.map(lambda _: VMEM, outs),
        scratch_shapes=scratch,
        compiler_params=pltpu.CompilerParams(vmem_limit_bytes=16 * 1024 * 1024),
        cost_estimate=pl.CostEstimate(
            flops=weight << 32, bytes_accessed=weight << 24, transcendentals=0
        ),
        name=name,
    )(*(pltpu.with_memory_space_constraint(a, pltpu.VMEM) for a in operands))


def in_vmem(a):
    return pltpu.VMEM(a.shape, a.dtype)


def ids_kernel(out_ref):
    out_ref[...] = lax.broadcasted_iota(jnp.int32, out_ref.shape, 0)


def request_kernel(total_lags, shift, slab_shift, ids_ref, source_ref, offset_ref, delay_ref, code_ref):
    source = source_ref[...]
    chunk, lane = ids_ref.shape
    looked = jnp.zeros_like(source)
    for first in range(0, delay_ref.shape[1], chunk):
        delay = jnp.transpose(jnp.broadcast_to(delay_ref[:, first : first + chunk], (lane, chunk)))
        block = ids_ref[...] + first
        looked = looked + jnp.sum(jnp.where(block == source, delay, 0), axis=0, keepdims=True)
    lag = offset_ref[...] + looked
    lag = jnp.where(lag >= total_lags, lag - total_lags, lag)
    code_ref[:, :lane] = (lag << shift) | source
    owner = source >> slab_shift
    other = jnp.transpose(jnp.broadcast_to(owner, (lane, lane)))
    earlier = lax.broadcasted_iota(jnp.int32, (lane, lane), 0) < lax.broadcasted_iota(
        jnp.int32, (lane, lane), 1
    )
    alike = jnp.where((other == owner) & earlier, 1, 0)
    code_ref[:, lane:] = jnp.sum(alike, axis=0, keepdims=True)


def join_kernel(mine_ref, other_ref, out_ref):
    rows = mine_ref.shape[0]
    out_ref[:rows] = mine_ref[...]
    out_ref[rows:] = other_ref[...]


def ordinal(plan, piece, lag):
    if not plan.split:
        return jnp.where(piece < plan.pieces, piece, -1)
    low, high = plan.split
    turn = jnp.where(lag == 0, low, high)
    return jnp.where(
        piece == 0, 0, jnp.where(piece == turn, 1, jnp.where(piece == low + high, 2, -1))
    )


def select_kernel(plan, groups, near_ref, far_ref, near_pieces_ref, far_pieces_ref, *out_refs):
    size, cap, lag_shift = plan.size, plan.cap, plan.lag_shift
    blk, lag = lax.axis_index("blk"), lax.axis_index("lag")
    slabs = [r[q] for r in (near_pieces_ref, far_pieces_ref) for q in range(r.shape[0])]
    width = slabs[0].shape[1]
    table = [s[:, b : b + size] for s in slabs for b in range(0, width, size)]
    table = jnp.concatenate(
        [jnp.concatenate(table[: len(table) // 2]), jnp.concatenate(table[len(table) // 2 :])], axis=1
    )
    depth = table.shape[0]
    code = jnp.concatenate([near_ref[...], far_ref[...]], axis=0)
    tiles = code.shape[1] // 2
    address, place = code[:, :tiles], code[:, tiles:]
    source = address & ((1 << plan.shift) - 1)
    wanted = address >> plan.shift
    piece = (source >> plan.slab_shift) ^ blk
    half = wanted >> lag_shift
    if plan.split:
        low, high = plan.split
        same, turn = half == lag, jnp.where(lag == 0, low, high)
        slab = jnp.where((piece == 0) & same, 0, -1)
        slab = jnp.where(piece == turn, jnp.where(same, 1, 2), slab)
        slab = jnp.where((piece == low + high) & jnp.logical_not(same), 3, slab)
    else:
        slab = jnp.where((piece < plan.pieces) & (half == lag), piece, -1)
    inner = (source & ((1 << plan.slab_shift) - 1)) << lag_shift
    row = (slab << (plan.slab_shift + lag_shift)) + inner + (wanted & ((1 << lag_shift) - 1))
    row = jnp.where(slab >= 0, row, -1)
    rank = ordinal(plan, piece, lag)
    slot = jnp.where(rank >= 0, rank * cap + place, -1)

    def picked(chosen):
        lane = lax.broadcasted_iota(jnp.int32, chosen.shape, 1)
        low = chosen & (depth - 1)
        onehot = jnp.concatenate(
            [
                jnp.where(low == lane + first, 1.0, 0.0).astype(jnp.bfloat16)
                for first in range(0, depth, size)
            ],
            axis=1,
        )
        both = jnp.dot(onehot, table, preferred_element_type=jnp.float32)
        upper = chosen >> (depth.bit_length() - 1)
        rows = jnp.where(upper == 0, both[:, :size], jnp.where(upper == 1, both[:, size:], 0.0))
        return rows.astype(jnp.bfloat16)

    slot_id = lax.broadcasted_iota(jnp.int32, (plan.slots, tiles), 0)
    for group, out_ref in zip(groups, out_refs):
        for k, d in enumerate(group):
            there = jnp.where(slot_id == slot[d : d + 1], row[d : d + 1] + 1, 0)
            chosen = jnp.sum(there, axis=1, keepdims=True) - 1
            chosen = jnp.broadcast_to(chosen, (plan.slots, size))
            out_ref[k * plan.slots : (k + 1) * plan.slots, :] = picked(chosen)


def order_kernel(
    plan, hops, count, code_ref, target_ref, held_ref, tiles_ref, passed_ref, tile_ref, column_ref, turned_ref, *scratch
):
    tiles, size = tiles_ref.shape[:2]
    passed_ref[...] = held_ref[...]
    blk, lag = lax.axis_index("blk"), lax.axis_index("lag")
    source = code_ref[:, :tiles] & ((1 << plan.shift) - 1)
    place = code_ref[:, tiles:]
    apart = (source >> plan.slab_shift) ^ blk
    piece, high = apart & (plan.pieces - 1), apart >> (plan.pieces.bit_length() - 1)
    plane = sum(((high >> (hops - 1 - i)) & 1) << i for i in range(hops))
    sender = jnp.zeros_like(plane) + lag
    if plan.split:
        for i in range(hops):
            sender = sender ^ ((plane >> i) & 1)
    rank = ordinal(plan, piece, sender)
    slot = jnp.where(rank >= 0, plane * plan.slots + rank * plan.cap + place, -1)
    wide = tile_ref.shape[1]
    slot = jnp.transpose(jnp.broadcast_to(slot, (wide, tiles)))
    target = jnp.transpose(jnp.broadcast_to(target_ref[...], (wide, tiles)))
    here = slot == lax.broadcasted_iota(jnp.int32, (tiles, wide), 1)
    tile = jnp.where(here, lax.broadcasted_iota(jnp.int32, (tiles, wide), 0), 0)
    tile_ref[...] = jnp.minimum(jnp.sum(tile, axis=0, keepdims=True), tiles - 1)
    target = jnp.sum(jnp.where(here, target + 1, 0), axis=0, keepdims=True) - 1
    column_ref[...] = jnp.transpose(jnp.broadcast_to(target, (size, wide)))[: column_ref.shape[0], :]
    turn(0, count, tile_ref, tiles_ref, turned_ref, *scratch)


def turn(first, count, tile_ref, tiles_ref, turned_ref, index, sem):
    copy = pltpu.make_async_copy(tile_ref, index, sem)
    copy.start()
    copy.wait()
    size = tiles_ref.shape[1]
    for s in range(count):
        turned_ref[s * size : (s + 1) * size, :] = jnp.transpose(tiles_ref[index[0, first + s]])


def turn_kernel(first, count, held_ref, tile_ref, tiles_ref, passed_ref, turned_ref, *scratch):
    passed_ref[...] = held_ref[...]
    turn(first, count, tile_ref, tiles_ref, turned_ref, *scratch)


def products(first, column_ref, row_refs, turned_refs, blocks):
    rows = jnp.concatenate([r[...] for r in row_refs], axis=0).astype(jnp.float32)
    count, size = rows.shape
    target = column_ref[first : first + count, :]
    left = jnp.stack([jnp.where(target == b, rows, 0.0) for b in range(blocks)], axis=0)
    left = left.astype(jnp.bfloat16)
    total = jnp.zeros((blocks, size), jnp.float32)
    for turned_ref, start, held in turned_refs:
        low, high = max(first, start), min(first + count, start + held)
        if low < high:
            part = left[:, low - first : high - first].reshape(blocks, (high - low) * size)
            total = total + jnp.dot(
                part,
                turned_ref[(low - start) * size : (high - start) * size, :],
                preferred_element_type=jnp.float32,
            )
    return total


def early_kernel(cuts, n_rows, column_ref, tile_ref, tiles_ref, turned0_ref, turned1_ref, *refs):
    row_refs, (sum_ref, turned_ref, index, sem) = refs[:n_rows], refs[n_rows:]
    turned = [(turned0_ref, cuts[0], cuts[1] - cuts[0]), (turned1_ref, cuts[1], cuts[2] - cuts[1])]
    sum_ref[...] = products(0, column_ref, row_refs, turned, sum_ref.shape[0])
    turn(cuts[2], cuts[3] - cuts[2], tile_ref, tiles_ref, turned_ref, index, sem)


def couple_kernel(cuts, early_ref, column_ref, turned1_ref, turned2_ref, rows_ref, out_ref):
    turned = [(turned1_ref, cuts[1], cuts[2] - cuts[1]), (turned2_ref, cuts[2], cuts[3] - cuts[2])]
    first = cuts[3] - rows_ref.shape[0]
    out_ref[...] = early_ref[...] + products(first, column_ref, [rows_ref], turned, out_ref.shape[0])


def solve_kernel(mine_ref, other_ref, incident_ref, inverse_ref, out_ref):
    blocks, size = incident_ref.shape
    excite = incident_ref[...] - (mine_ref[...] + other_ref[...])
    lane = lax.broadcasted_iota(jnp.int32, (size, blocks), 1)
    solved = jnp.zeros((size, blocks), jnp.float32)
    for b in range(blocks):
        product = inverse_ref[b] * jnp.broadcast_to(excite[b : b + 1, :], (size, size))
        solved = jnp.where(lane == b, jnp.sum(product, axis=1, keepdims=True), solved)
    out_ref[...] = jnp.transpose(solved)


def body(
    history, tile_blocks, tile_target, tile_source, tile_offset, delay_bins, incident, self_inv
):
    lag_rows = history.shape[0]
    tile_count, size = tile_blocks.shape[:2]
    slab_blocks = self_inv.shape[0]
    n_blk, n_lag = lax.axis_size("blk"), lax.axis_size("lag")
    all_blocks = delay_bins.shape[0]
    bits = n_blk.bit_length() - 1
    shift = all_blocks.bit_length() - 1
    slab_shift = slab_blocks.bit_length() - 1
    gather_bits = [1 << i for i in range(bits // 2)]
    exchange_bits = [1 << i for i in range(bits - 1, bits // 2 - 1, -1)]
    lag_shift = lag_rows.bit_length() - 1
    paired = n_lag == 2 and len(gather_bits) == 2
    cap = 2 * tile_count // n_blk
    n_pieces = 1 << len(gather_bits)
    plan = Plan(
        size,
        slab_shift,
        shift,
        lag_shift,
        n_pieces,
        cap,
        (3 if paired else n_pieces) * cap,
        tuple(gather_bits) if paired else (),
    )

    def hop(value, bit, other=None, flip=1):
        bits_of, flip = [bit, bit if other is None else other], flip if paired else 0
        pairs = [
            (j * n_lag + c, (j ^ bits_of[c % 2]) * n_lag + (c ^ flip))
            for j in range(n_blk)
            for c in range(n_lag)
        ]
        return lax.ppermute(value, ("blk", "lag"), pairs)

    if paired:
        first = hop(history[None], *gather_bits, flip=0)
    else:
        first = hop(history[None], gather_bits[0])
    ids = call(ids_kernel, "ids", pltpu.VMEM((min(all_blocks, 128), tile_count), jnp.int32), weight=8)
    code = call(
        lambda *refs: request_kernel(lag_rows * n_lag, shift, slab_shift, *refs),
        "request",
        pltpu.VMEM((1, 2 * tile_count), jnp.int32),
        ids,
        tile_source[None],
        tile_offset[None],
        delay_bins[None],
        weight=0,
    )

    def join(name, mine, other, weight, *extra):
        shape = (2 * mine.shape[0],) + mine.shape[1:]
        return call(
            lambda *refs: join_kernel(refs[0], refs[1], refs[-1]),
            name,
            pltpu.VMEM(shape, mine.dtype),
            mine,
            other,
            *extra,
            weight=weight,
        )

    own_code = code
    for bit in exchange_bits[:-1]:
        code = join("join", code, hop(code, bit), 8)
    far_code = hop(code, exchange_bits[-1])
    pieces, arrived = history[None], first
    for bit in gather_bits[1:]:
        pieces = join("gather", pieces, arrived, 0, tile_blocks)
        arrived = hop(pieces, bit, gather_bits[0]) if paired else hop(pieces, bit)

    n_hops = len(exchange_bits)

    n_slots = plan.slots << n_hops
    cuts = [0, n_slots // 64 * 16, max(n_slots // 2, n_slots * 7 // 12 // 16 * 16), n_slots]
    wide = -(-n_slots // 128) * 128
    scratch = [pltpu.SMEM((1, wide), jnp.int32), pltpu.SemaphoreType.DMA]

    def turned_tiles(run):
        return pltpu.VMEM(((cuts[run + 1] - cuts[run]) * size, size), tile_blocks.dtype)

    code, slot_tiles, columns, turned0 = call(
        lambda *refs: order_kernel(plan, n_hops, cuts[1], *refs),
        "order",
        (in_vmem(code), pltpu.VMEM((1, wide), jnp.int32), pltpu.VMEM((n_slots, size), jnp.int32), turned_tiles(0)),
        own_code,
        tile_target[None],
        code,
        tile_blocks,
        weight=0,
        scratch=scratch,
    )

    def select(name, groups, rows, weight, *after):
        return call(
            lambda *refs: select_kernel(plan, groups, *refs[len(after) :]),
            name,
            [pltpu.VMEM((n, size), jnp.bfloat16) for n in rows],
            *after,
            code,
            far_code,
            pieces,
            arrived,
            weight=weight,
        )

    def passes(i):
        return [d for d in range(1 << n_hops) if d >> i > 1 and (d >> i) & 1 and d % (1 << i) == 0]

    first_pass = passes(0) + [1]
    (send,) = select("select_send", [first_pass], [plan.slots * len(first_pass)], 16)
    rest = [d for d in range(2, 1 << n_hops) if d % 2 == 0]
    *picks, keep = select("select_keep", [[d] for d in rest + [0]], [plan.slots] * (len(rest) + 1), 16, send)
    held = dict(zip(rest, picks))
    keep, turned1 = call(
        lambda *refs: turn_kernel(cuts[1], cuts[2] - cuts[1], *refs),
        "turn",
        (in_vmem(keep), turned_tiles(1)),
        keep,
        slot_tiles,
        tile_blocks,
        weight=4,
        scratch=scratch,
    )
    landed = []
    for i, bit in enumerate(exchange_bits):
        onward, rows = passes(i), plan.slots << i
        if onward:
            if i:
                send = jnp.concatenate([held[d] for d in onward + [1 << i]], axis=0)
            passed = hop(send, bit)
            landed.append(passed[len(onward) * rows :])
        if i == n_hops - 1:
            early, turned2 = call(
                lambda *refs: early_kernel(cuts, n_hops, *refs),
                "early",
                (pltpu.VMEM((slab_blocks, size), jnp.float32), turned_tiles(2)),
                columns,
                slot_tiles,
                tile_blocks,
                turned0,
                turned1,
                keep,
                *landed,
                weight=4,
                scratch=scratch,
            )
        if not onward:
            landed.append(hop(held[1 << i], bit))
        for k, d in enumerate(onward):
            here = d ^ (1 << i)
            held[here] = jnp.concatenate([held[here], passed[k * rows : (k + 1) * rows]], axis=0)
    mine = call(
        lambda *refs: couple_kernel(cuts, *refs),
        "couple",
        pltpu.VMEM((slab_blocks, size), jnp.float32),
        early,
        columns,
        turned1,
        turned2,
        landed[-1],
    )
    if n_lag == 2:
        other = lax.ppermute(mine, "lag", [(0, 1), (1, 0)])
    else:
        other = lax.psum(mine, "lag") - mine
    solved = call(
        solve_kernel,
        "solve",
        jax.ShapeDtypeStruct((slab_blocks, size), jnp.float32),
        mine,
        other,
        incident.reshape(slab_blocks, size),
        self_inv,
    )
    return solved.reshape(slab_blocks * size)


def solution(mesh):
    return jax.shard_map(
        body,
        mesh=mesh,
        in_specs=(
            P("lag", "blk"),
            P("blk", None, None),
            P("blk"),
            P("blk"),
            P("blk"),
            P(),
            P("blk"),
            P("blk", None, None),
        ),
        out_specs=P("blk"),
        check_vma=False,
    )
```

```python
import typing

import jax
import jax.numpy as jnp
from jax import lax
from jax.experimental import pallas as pl
from jax.experimental.pallas import tpu as pltpu
from jax.sharding import PartitionSpec as P


VMEM = pl.BlockSpec(memory_space=pltpu.VMEM)


class Plan(typing.NamedTuple):
    size: int
    slab_shift: int
    shift: int
    lag_shift: int
    pieces: int
    cap: int
    slots: int
    split: tuple


def call(kernel, name, outs, *operands, weight=0, scratch=()):
    return pl.pallas_call(
        kernel,
        out_shape=outs,
        in_specs=[VMEM] * len(operands),
        out_specs=jax.tree.map(lambda _: VMEM, outs),
        scratch_shapes=scratch,
        compiler_params=pltpu.CompilerParams(vmem_limit_bytes=16 * 1024 * 1024),
        cost_estimate=pl.CostEstimate(
            flops=weight << 32, bytes_accessed=weight << 24, transcendentals=0
        ),
        name=name,
    )(*(pltpu.with_memory_space_constraint(a, pltpu.VMEM) for a in operands))


def in_vmem(a):
    return pltpu.VMEM(a.shape, a.dtype)


def ids_kernel(out_ref):
    out_ref[...] = lax.broadcasted_iota(jnp.int32, out_ref.shape, 0)


def request_kernel(total_lags, shift, slab_shift, ids_ref, source_ref, offset_ref, delay_ref, code_ref):
    source = source_ref[...]
    chunk, lane = ids_ref.shape
    looked = jnp.zeros_like(source)
    for first in range(0, delay_ref.shape[1], chunk):
        delay = jnp.transpose(jnp.broadcast_to(delay_ref[:, first : first + chunk], (lane, chunk)))
        block = ids_ref[...] + first
        looked = looked + jnp.sum(jnp.where(block == source, delay, 0), axis=0, keepdims=True)
    lag = offset_ref[...] + looked
    lag = jnp.where(lag >= total_lags, lag - total_lags, lag)
    code_ref[:, :lane] = (lag << shift) | source
    owner = source >> slab_shift
    other = jnp.transpose(jnp.broadcast_to(owner, (lane, lane)))
    earlier = lax.broadcasted_iota(jnp.int32, (lane, lane), 0) < lax.broadcasted_iota(
        jnp.int32, (lane, lane), 1
    )
    alike = jnp.where((other == owner) & earlier, 1, 0)
    code_ref[:, lane:] = jnp.sum(alike, axis=0, keepdims=True)


def join_kernel(mine_ref, other_ref, out_ref):
    rows = mine_ref.shape[0]
    out_ref[:rows] = mine_ref[...]
    out_ref[rows:] = other_ref[...]


def ordinal(plan, piece, lag):
    if not plan.split:
        return jnp.where(piece < plan.pieces, piece, -1)
    low, high = plan.split
    turn = jnp.where(lag == 0, low, high)
    return jnp.where(
        piece == 0, 0, jnp.where(piece == turn, 1, jnp.where(piece == low + high, 2, -1))
    )


def select_kernel(plan, groups, near_ref, far_ref, near_pieces_ref, far_pieces_ref, *out_refs):
    size, cap, lag_shift = plan.size, plan.cap, plan.lag_shift
    blk, lag = lax.axis_index("blk"), lax.axis_index("lag")
    slabs = [r[q] for r in (near_pieces_ref, far_pieces_ref) for q in range(r.shape[0])]
    width = slabs[0].shape[1]
    table = [s[:, b : b + size] for s in slabs for b in range(0, width, size)]
    table = jnp.concatenate(
        [jnp.concatenate(table[: len(table) // 2]), jnp.concatenate(table[len(table) // 2 :])], axis=1
    )
    depth = table.shape[0]
    code = jnp.concatenate([near_ref[...], far_ref[...]], axis=0)
    tiles = code.shape[1] // 2
    address, place = code[:, :tiles], code[:, tiles:]
    source = address & ((1 << plan.shift) - 1)
    wanted = address >> plan.shift
    piece = (source >> plan.slab_shift) ^ blk
    half = wanted >> lag_shift
    if plan.split:
        low, high = plan.split
        same, turn = half == lag, jnp.where(lag == 0, low, high)
        slab = jnp.where((piece == 0) & same, 0, -1)
        slab = jnp.where(piece == turn, jnp.where(same, 1, 2), slab)
        slab = jnp.where((piece == low + high) & jnp.logical_not(same), 3, slab)
    else:
        slab = jnp.where((piece < plan.pieces) & (half == lag), piece, -1)
    inner = (source & ((1 << plan.slab_shift) - 1)) << lag_shift
    row = (slab << (plan.slab_shift + lag_shift)) + inner + (wanted & ((1 << lag_shift) - 1))
    row = jnp.where(slab >= 0, row, -1)
    rank = ordinal(plan, piece, lag)
    slot = jnp.where(rank >= 0, rank * cap + place, -1)

    def picked(chosen):
        lane = lax.broadcasted_iota(jnp.int32, chosen.shape, 1)
        low = chosen & (depth - 1)
        onehot = jnp.concatenate(
            [
                jnp.where(low == lane + first, 1.0, 0.0).astype(jnp.bfloat16)
                for first in range(0, depth, size)
            ],
            axis=1,
        )
        both = jnp.dot(onehot, table, preferred_element_type=jnp.float32)
        upper = chosen >> (depth.bit_length() - 1)
        rows = jnp.where(upper == 0, both[:, :size], jnp.where(upper == 1, both[:, size:], 0.0))
        return rows.astype(jnp.bfloat16)

    slot_id = lax.broadcasted_iota(jnp.int32, (plan.slots, tiles), 0)
    for group, out_ref in zip(groups, out_refs):
        for k, d in enumerate(group):
            there = jnp.where(slot_id == slot[d : d + 1], row[d : d + 1] + 1, 0)
            chosen = jnp.sum(there, axis=1, keepdims=True) - 1
            chosen = jnp.broadcast_to(chosen, (plan.slots, size))
            out_ref[k * plan.slots : (k + 1) * plan.slots, :] = picked(chosen)


def order_kernel(
    plan, hops, count, code_ref, target_ref, held_ref, tiles_ref, passed_ref, tile_ref, column_ref, turned_ref, *scratch
):
    tiles, size = tiles_ref.shape[:2]
    passed_ref[...] = held_ref[...]
    blk, lag = lax.axis_index("blk"), lax.axis_index("lag")
    source = code_ref[:, :tiles] & ((1 << plan.shift) - 1)
    place = code_ref[:, tiles:]
    apart = (source >> plan.slab_shift) ^ blk
    piece, high = apart & (plan.pieces - 1), apart >> (plan.pieces.bit_length() - 1)
    plane = sum(((high >> (hops - 1 - i)) & 1) << i for i in range(hops))
    sender = jnp.zeros_like(plane) + lag
    if plan.split:
        for i in range(hops):
            sender = sender ^ ((plane >> i) & 1)
    rank = ordinal(plan, piece, sender)
    slot = jnp.where(rank >= 0, plane * plan.slots + rank * plan.cap + place, -1)
    wide = tile_ref.shape[1]
    slot = jnp.transpose(jnp.broadcast_to(slot, (wide, tiles)))
    target = jnp.transpose(jnp.broadcast_to(target_ref[...], (wide, tiles)))
    here = slot == lax.broadcasted_iota(jnp.int32, (tiles, wide), 1)
    tile = jnp.where(here, lax.broadcasted_iota(jnp.int32, (tiles, wide), 0), 0)
    tile_ref[...] = jnp.minimum(jnp.sum(tile, axis=0, keepdims=True), tiles - 1)
    target = jnp.sum(jnp.where(here, target + 1, 0), axis=0, keepdims=True) - 1
    column_ref[...] = jnp.transpose(jnp.broadcast_to(target, (size, wide)))[: column_ref.shape[0], :]
    turn(0, count, tile_ref, tiles_ref, turned_ref, *scratch)


def turn(first, count, tile_ref, tiles_ref, turned_ref, index, sem):
    copy = pltpu.make_async_copy(tile_ref, index, sem)
    copy.start()
    copy.wait()
    size = tiles_ref.shape[1]
    for s in range(count):
        turned_ref[s * size : (s + 1) * size, :] = jnp.transpose(tiles_ref[index[0, first + s]])


def turn_kernel(first, count, held_ref, tile_ref, tiles_ref, passed_ref, turned_ref, *scratch):
    passed_ref[...] = held_ref[...]
    turn(first, count, tile_ref, tiles_ref, turned_ref, *scratch)


def products(first, column_ref, row_refs, turned_refs, blocks):
    rows = jnp.concatenate([r[...] for r in row_refs], axis=0).astype(jnp.float32)
    count, size = rows.shape
    target = column_ref[first : first + count, :]
    left = jnp.stack([jnp.where(target == b, rows, 0.0) for b in range(blocks)], axis=0)
    left = left.astype(jnp.bfloat16)
    total = jnp.zeros((blocks, size), jnp.float32)
    for turned_ref, start, held in turned_refs:
        low, high = max(first, start), min(first + count, start + held)
        if low < high:
            part = left[:, low - first : high - first].reshape(blocks, (high - low) * size)
            total = total + jnp.dot(
                part,
                turned_ref[(low - start) * size : (high - start) * size, :],
                preferred_element_type=jnp.float32,
            )
    return total


def early_kernel(
    cuts, n_rows, column_ref, tile_ref, tiles_ref, inverse_ref, turned0_ref, turned1_ref, *refs
):
    row_refs, (sum_ref, turned_ref, high_ref, low_ref, index, sem) = refs[:n_rows], refs[n_rows:]
    turned = [(turned0_ref, cuts[0], cuts[1] - cuts[0]), (turned1_ref, cuts[1], cuts[2] - cuts[1])]
    sum_ref[...] = products(0, column_ref, row_refs, turned, sum_ref.shape[0])
    turn(cuts[2], cuts[3] - cuts[2], tile_ref, tiles_ref, turned_ref, index, sem)
    blocks, size = inverse_ref.shape[:2]
    for b in range(blocks):
        whole = jnp.transpose(inverse_ref[b])
        high = whole.astype(jnp.bfloat16)
        high_ref[b * size : (b + 1) * size, :] = high
        low = whole - high.astype(jnp.float32)
        low_ref[b * size : (b + 1) * size, :] = low.astype(jnp.bfloat16)


def couple_kernel(cuts, early_ref, column_ref, turned1_ref, turned2_ref, rows_ref, out_ref):
    turned = [(turned1_ref, cuts[1], cuts[2] - cuts[1]), (turned2_ref, cuts[2], cuts[3] - cuts[2])]
    first = cuts[3] - rows_ref.shape[0]
    out_ref[...] = early_ref[...] + products(first, column_ref, [rows_ref], turned, out_ref.shape[0])


def solve_kernel(mine_ref, other_ref, incident_ref, high_ref, low_ref, out_ref):
    blocks, size = incident_ref.shape
    excite = incident_ref[...] - (mine_ref[...] + other_ref[...])
    high = excite.astype(jnp.bfloat16).astype(jnp.float32)
    block_id = lax.broadcasted_iota(jnp.int32, (blocks, size), 0)

    def spread(rows):
        parts = [jnp.where(block_id == b, rows, 0.0) for b in range(blocks)]
        return jnp.concatenate(parts, axis=1)

    left = jnp.concatenate([spread(high), spread(excite - high)], axis=0).astype(jnp.bfloat16)
    first = jnp.dot(left, high_ref[...], preferred_element_type=jnp.float32)
    second = jnp.dot(left, low_ref[...], preferred_element_type=jnp.float32)
    out_ref[...] = first[:blocks] + (first[blocks:] + second[:blocks])


def body(
    history, tile_blocks, tile_target, tile_source, tile_offset, delay_bins, incident, self_inv
):
    lag_rows = history.shape[0]
    tile_count, size = tile_blocks.shape[:2]
    slab_blocks = self_inv.shape[0]
    n_blk, n_lag = lax.axis_size("blk"), lax.axis_size("lag")
    all_blocks = delay_bins.shape[0]
    bits = n_blk.bit_length() - 1
    shift = all_blocks.bit_length() - 1
    slab_shift = slab_blocks.bit_length() - 1
    gather_bits = [1 << i for i in range(bits // 2)]
    exchange_bits = [1 << i for i in range(bits - 1, bits // 2 - 1, -1)]
    lag_shift = lag_rows.bit_length() - 1
    paired = n_lag == 2 and len(gather_bits) == 2
    cap = 2 * tile_count // n_blk
    n_pieces = 1 << len(gather_bits)
    plan = Plan(
        size,
        slab_shift,
        shift,
        lag_shift,
        n_pieces,
        cap,
        (3 if paired else n_pieces) * cap,
        tuple(gather_bits) if paired else (),
    )

    def hop(value, bit, other=None, flip=1):
        bits_of, flip = [bit, bit if other is None else other], flip if paired else 0
        pairs = [
            (j * n_lag + c, (j ^ bits_of[c % 2]) * n_lag + (c ^ flip))
            for j in range(n_blk)
            for c in range(n_lag)
        ]
        return lax.ppermute(value, ("blk", "lag"), pairs)

    if paired:
        first = hop(history[None], *gather_bits, flip=0)
    else:
        first = hop(history[None], gather_bits[0])
    ids = call(ids_kernel, "ids", pltpu.VMEM((min(all_blocks, 128), tile_count), jnp.int32), weight=8)
    code = call(
        lambda *refs: request_kernel(lag_rows * n_lag, shift, slab_shift, *refs),
        "request",
        pltpu.VMEM((1, 2 * tile_count), jnp.int32),
        ids,
        tile_source[None],
        tile_offset[None],
        delay_bins[None],
        weight=0,
    )

    def join(name, mine, other, weight, *extra):
        shape = (2 * mine.shape[0],) + mine.shape[1:]
        return call(
            lambda *refs: join_kernel(refs[0], refs[1], refs[-1]),
            name,
            pltpu.VMEM(shape, mine.dtype),
            mine,
            other,
            *extra,
            weight=weight,
        )

    own_code = code
    for bit in exchange_bits[:-1]:
        code = join("join", code, hop(code, bit), 8)
    far_code = hop(code, exchange_bits[-1])
    pieces, arrived = history[None], first
    for bit in gather_bits[1:]:
        pieces = join("gather", pieces, arrived, 0, tile_blocks)
        arrived = hop(pieces, bit, gather_bits[0]) if paired else hop(pieces, bit)

    n_hops = len(exchange_bits)

    n_slots = plan.slots << n_hops
    cuts = [0, n_slots // 64 * 16, max(n_slots // 2, n_slots * 7 // 12 // 16 * 16), n_slots]
    wide = -(-n_slots // 128) * 128
    scratch = [pltpu.SMEM((1, wide), jnp.int32), pltpu.SemaphoreType.DMA]

    def turned_tiles(run):
        return pltpu.VMEM(((cuts[run + 1] - cuts[run]) * size, size), tile_blocks.dtype)

    code, slot_tiles, columns, turned0 = call(
        lambda *refs: order_kernel(plan, n_hops, cuts[1], *refs),
        "order",
        (in_vmem(code), pltpu.VMEM((1, wide), jnp.int32), pltpu.VMEM((n_slots, size), jnp.int32), turned_tiles(0)),
        own_code,
        tile_target[None],
        code,
        tile_blocks,
        weight=0,
        scratch=scratch,
    )

    def select(name, groups, rows, weight, *after):
        return call(
            lambda *refs: select_kernel(plan, groups, *refs[len(after) :]),
            name,
            [pltpu.VMEM((n, size), jnp.bfloat16) for n in rows],
            *after,
            code,
            far_code,
            pieces,
            arrived,
            weight=weight,
        )

    def passes(i):
        return [d for d in range(1 << n_hops) if d >> i > 1 and (d >> i) & 1 and d % (1 << i) == 0]

    first_pass = passes(0) + [1]
    (send,) = select("select_send", [first_pass], [plan.slots * len(first_pass)], 16)
    rest = [d for d in range(2, 1 << n_hops) if d % 2 == 0]
    *picks, keep = select("select_keep", [[d] for d in rest + [0]], [plan.slots] * (len(rest) + 1), 16, send)
    held = dict(zip(rest, picks))
    keep, turned1 = call(
        lambda *refs: turn_kernel(cuts[1], cuts[2] - cuts[1], *refs),
        "turn",
        (in_vmem(keep), turned_tiles(1)),
        keep,
        slot_tiles,
        tile_blocks,
        weight=4,
        scratch=scratch,
    )
    landed = []
    for i, bit in enumerate(exchange_bits):
        onward, rows = passes(i), plan.slots << i
        if onward:
            if i:
                send = jnp.concatenate([held[d] for d in onward + [1 << i]], axis=0)
            passed = hop(send, bit)
            landed.append(passed[len(onward) * rows :])
        if i == n_hops - 1:
            inverse = pltpu.VMEM((slab_blocks * size, size), jnp.bfloat16)
            early, turned2, *inverses = call(
                lambda *refs: early_kernel(cuts, n_hops, *refs),
                "early",
                (pltpu.VMEM((slab_blocks, size), jnp.float32), turned_tiles(2), inverse, inverse),
                columns,
                slot_tiles,
                tile_blocks,
                self_inv,
                turned0,
                turned1,
                keep,
                *landed,
                weight=4,
                scratch=scratch,
            )
        if not onward:
            landed.append(hop(held[1 << i], bit))
        for k, d in enumerate(onward):
            here = d ^ (1 << i)
            held[here] = jnp.concatenate([held[here], passed[k * rows : (k + 1) * rows]], axis=0)
    mine = call(
        lambda *refs: couple_kernel(cuts, *refs),
        "couple",
        pltpu.VMEM((slab_blocks, size), jnp.float32),
        early,
        columns,
        turned1,
        turned2,
        landed[-1],
    )
    if n_lag == 2:
        other = lax.ppermute(mine, "lag", [(0, 1), (1, 0)])
    else:
        other = lax.psum(mine, "lag") - mine
    solved = call(
        solve_kernel,
        "solve",
        jax.ShapeDtypeStruct((slab_blocks, size), jnp.float32),
        mine,
        other,
        incident.reshape(slab_blocks, size),
        *inverses,
    )
    return solved.reshape(slab_blocks * size)


def solution(mesh):
    return jax.shard_map(
        body,
        mesh=mesh,
        in_specs=(
            P("lag", "blk"),
            P("blk", None, None),
            P("blk"),
            P("blk"),
            P("blk"),
            P(),
            P("blk"),
            P("blk", None, None),
        ),
        out_specs=P("blk"),
        check_vma=False,
    )
```

```python
import typing

import jax
import jax.numpy as jnp
from jax import lax
from jax.experimental import pallas as pl
from jax.experimental.pallas import tpu as pltpu
from jax.sharding import PartitionSpec as P


VMEM = pl.BlockSpec(memory_space=pltpu.VMEM)


class Plan(typing.NamedTuple):
    size: int
    slab_shift: int
    shift: int
    lag_shift: int
    pieces: int
    cap: int
    slots: int
    split: tuple


def call(kernel, name, outs, *operands, weight=0, scratch=()):
    return pl.pallas_call(
        kernel,
        out_shape=outs,
        in_specs=[VMEM] * len(operands),
        out_specs=jax.tree.map(lambda _: VMEM, outs),
        scratch_shapes=scratch,
        compiler_params=pltpu.CompilerParams(vmem_limit_bytes=16 * 1024 * 1024),
        cost_estimate=pl.CostEstimate(
            flops=weight << 32, bytes_accessed=weight << 24, transcendentals=0
        ),
        name=name,
    )(*(pltpu.with_memory_space_constraint(a, pltpu.VMEM) for a in operands))


def in_vmem(a):
    return pltpu.VMEM(a.shape, a.dtype)


def ids_kernel(out_ref):
    out_ref[...] = lax.broadcasted_iota(jnp.int32, out_ref.shape, 0)


def request_kernel(total_lags, shift, slab_shift, ids_ref, source_ref, offset_ref, delay_ref, code_ref):
    source = source_ref[...]
    chunk, lane = ids_ref.shape
    looked = jnp.zeros_like(source)
    for first in range(0, delay_ref.shape[1], chunk):
        delay = jnp.transpose(jnp.broadcast_to(delay_ref[:, first : first + chunk], (lane, chunk)))
        block = ids_ref[...] + first
        looked = looked + jnp.sum(jnp.where(block == source, delay, 0), axis=0, keepdims=True)
    lag = offset_ref[...] + looked
    lag = jnp.where(lag >= total_lags, lag - total_lags, lag)
    code_ref[:, :lane] = (lag << shift) | source
    owner = source >> slab_shift
    other = jnp.transpose(jnp.broadcast_to(owner, (lane, lane)))
    earlier = lax.broadcasted_iota(jnp.int32, (lane, lane), 0) < lax.broadcasted_iota(
        jnp.int32, (lane, lane), 1
    )
    alike = jnp.where((other == owner) & earlier, 1, 0)
    code_ref[:, lane:] = jnp.sum(alike, axis=0, keepdims=True)


def join_kernel(mine_ref, other_ref, out_ref):
    rows = mine_ref.shape[0]
    out_ref[:rows] = mine_ref[...]
    out_ref[rows:] = other_ref[...]


def ordinal(plan, piece, lag):
    if not plan.split:
        return jnp.where(piece < plan.pieces, piece, -1)
    low, high = plan.split
    turn = jnp.where(lag == 0, low, high)
    return jnp.where(
        piece == 0, 0, jnp.where(piece == turn, 1, jnp.where(piece == low + high, 2, -1))
    )


def select_kernel(plan, groups, near_ref, far_ref, near_pieces_ref, far_pieces_ref, *out_refs):
    size, cap, lag_shift = plan.size, plan.cap, plan.lag_shift
    blk, lag = lax.axis_index("blk"), lax.axis_index("lag")
    slabs = [r[q] for r in (near_pieces_ref, far_pieces_ref) for q in range(r.shape[0])]
    width = slabs[0].shape[1]
    table = [s[:, b : b + size] for s in slabs for b in range(0, width, size)]
    table = jnp.concatenate(
        [jnp.concatenate(table[: len(table) // 2]), jnp.concatenate(table[len(table) // 2 :])], axis=1
    )
    depth = table.shape[0]
    code = jnp.concatenate([near_ref[...], far_ref[...]], axis=0)
    tiles = code.shape[1] // 2
    address, place = code[:, :tiles], code[:, tiles:]
    source = address & ((1 << plan.shift) - 1)
    wanted = address >> plan.shift
    piece = (source >> plan.slab_shift) ^ blk
    half = wanted >> lag_shift
    if plan.split:
        low, high = plan.split
        same, turn = half == lag, jnp.where(lag == 0, low, high)
        slab = jnp.where((piece == 0) & same, 0, -1)
        slab = jnp.where(piece == turn, jnp.where(same, 1, 2), slab)
        slab = jnp.where((piece == low + high) & jnp.logical_not(same), 3, slab)
    else:
        slab = jnp.where((piece < plan.pieces) & (half == lag), piece, -1)
    inner = (source & ((1 << plan.slab_shift) - 1)) << lag_shift
    row = (slab << (plan.slab_shift + lag_shift)) + inner + (wanted & ((1 << lag_shift) - 1))
    row = jnp.where(slab >= 0, row, -1)
    rank = ordinal(plan, piece, lag)
    slot = jnp.where(rank >= 0, rank * cap + place, -1)

    def picked(chosen):
        lane = lax.broadcasted_iota(jnp.int32, chosen.shape, 1)
        low = chosen & (depth - 1)
        onehot = jnp.concatenate(
            [
                jnp.where(low == lane + first, 1.0, 0.0).astype(jnp.bfloat16)
                for first in range(0, depth, size)
            ],
            axis=1,
        )
        both = jnp.dot(onehot, table, preferred_element_type=jnp.float32)
        upper = chosen >> (depth.bit_length() - 1)
        rows = jnp.where(upper == 0, both[:, :size], jnp.where(upper == 1, both[:, size:], 0.0))
        return rows.astype(jnp.bfloat16)

    slot_id = lax.broadcasted_iota(jnp.int32, (plan.slots, tiles), 0)
    for group, out_ref in zip(groups, out_refs):
        for k, d in enumerate(group):
            there = jnp.where(slot_id == slot[d : d + 1], row[d : d + 1] + 1, 0)
            chosen = jnp.sum(there, axis=1, keepdims=True) - 1
            chosen = jnp.broadcast_to(chosen, (plan.slots, size))
            out_ref[k * plan.slots : (k + 1) * plan.slots, :] = picked(chosen)


def order_kernel(
    plan, hops, count, code_ref, target_ref, held_ref, tiles_ref, passed_ref, tile_ref, column_ref, turned_ref, *scratch
):
    tiles, size = tiles_ref.shape[:2]
    passed_ref[...] = held_ref[...]
    blk, lag = lax.axis_index("blk"), lax.axis_index("lag")
    source = code_ref[:, :tiles] & ((1 << plan.shift) - 1)
    place = code_ref[:, tiles:]
    apart = (source >> plan.slab_shift) ^ blk
    piece, high = apart & (plan.pieces - 1), apart >> (plan.pieces.bit_length() - 1)
    plane = sum(((high >> (hops - 1 - i)) & 1) << i for i in range(hops))
    sender = jnp.zeros_like(plane) + lag
    if plan.split:
        for i in range(hops):
            sender = sender ^ ((plane >> i) & 1)
    rank = ordinal(plan, piece, sender)
    slot = jnp.where(rank >= 0, plane * plan.slots + rank * plan.cap + place, -1)
    wide = tile_ref.shape[1]
    slot = jnp.transpose(jnp.broadcast_to(slot, (wide, tiles)))
    target = jnp.transpose(jnp.broadcast_to(target_ref[...], (wide, tiles)))
    here = slot == lax.broadcasted_iota(jnp.int32, (tiles, wide), 1)
    tile = jnp.where(here, lax.broadcasted_iota(jnp.int32, (tiles, wide), 0), 0)
    tile_ref[...] = jnp.minimum(jnp.sum(tile, axis=0, keepdims=True), tiles - 1)
    target = jnp.sum(jnp.where(here, target + 1, 0), axis=0, keepdims=True) - 1
    column_ref[...] = jnp.transpose(jnp.broadcast_to(target, (size, wide)))[: column_ref.shape[0], :]
    turn(0, count, tile_ref, tiles_ref, turned_ref, *scratch)


def turn(first, count, tile_ref, tiles_ref, turned_ref, index, sem):
    copy = pltpu.make_async_copy(tile_ref, index, sem)
    copy.start()
    copy.wait()
    size = tiles_ref.shape[1]
    for s in range(count):
        turned_ref[s * size : (s + 1) * size, :] = jnp.transpose(tiles_ref[index[0, first + s]])


def turn_kernel(first, count, held_ref, tile_ref, tiles_ref, passed_ref, turned_ref, *scratch):
    passed_ref[...] = held_ref[...]
    turn(first, count, tile_ref, tiles_ref, turned_ref, *scratch)


def products(first, column_ref, row_refs, turned_refs, blocks):
    rows = jnp.concatenate([r[...] for r in row_refs], axis=0).astype(jnp.float32)
    count, size = rows.shape
    target = column_ref[first : first + count, :]
    left = jnp.stack([jnp.where(target == b, rows, 0.0) for b in range(blocks)], axis=0)
    left = left.astype(jnp.bfloat16)
    total = jnp.zeros((blocks, size), jnp.float32)
    for turned_ref, start, held in turned_refs:
        low, high = max(first, start), min(first + count, start + held)
        if low < high:
            part = left[:, low - first : high - first].reshape(blocks, (high - low) * size)
            total = total + jnp.dot(
                part,
                turned_ref[(low - start) * size : (high - start) * size, :],
                preferred_element_type=jnp.float32,
            )
    return total


def early_kernel(
    cuts, n_rows, column_ref, tile_ref, tiles_ref, inverse_ref, turned0_ref, turned1_ref, *refs
):
    row_refs, (sum_ref, turned_ref, high_ref, low_ref, index, sem) = refs[:n_rows], refs[n_rows:]
    turned = [(turned0_ref, cuts[0], cuts[1] - cuts[0]), (turned1_ref, cuts[1], cuts[2] - cuts[1])]
    sum_ref[...] = products(0, column_ref, row_refs, turned, sum_ref.shape[0])
    turn(cuts[2], cuts[3] - cuts[2], tile_ref, tiles_ref, turned_ref, index, sem)
    blocks, size = inverse_ref.shape[:2]
    for b in range(blocks):
        whole = jnp.transpose(inverse_ref[b])
        high = whole.astype(jnp.bfloat16)
        high_ref[b * size : (b + 1) * size, :] = high
        low = whole - high.astype(jnp.float32)
        low_ref[b * size : (b + 1) * size, :] = low.astype(jnp.bfloat16)


def couple_kernel(cuts, early_ref, column_ref, turned1_ref, turned2_ref, rows_ref, out_ref):
    turned = [(turned1_ref, cuts[1], cuts[2] - cuts[1]), (turned2_ref, cuts[2], cuts[3] - cuts[2])]
    first = cuts[3] - rows_ref.shape[0]
    out_ref[...] = early_ref[...] + products(first, column_ref, [rows_ref], turned, out_ref.shape[0])


def solve_kernel(mine_ref, other_ref, incident_ref, high_ref, low_ref, out_ref):
    blocks, size = incident_ref.shape
    excite = incident_ref[...] - (mine_ref[...] + other_ref[...])
    high = excite.astype(jnp.bfloat16).astype(jnp.float32)
    block_id = lax.broadcasted_iota(jnp.int32, (blocks, size), 0)

    def spread(rows):
        parts = [jnp.where(block_id == b, rows, 0.0) for b in range(blocks)]
        return jnp.concatenate(parts, axis=1)

    left = jnp.concatenate([spread(high), spread(excite - high)], axis=0).astype(jnp.bfloat16)
    first = jnp.dot(left, high_ref[...], preferred_element_type=jnp.float32)
    second = jnp.dot(left, low_ref[...], preferred_element_type=jnp.float32)
    out_ref[...] = first[:blocks] + (first[blocks:] + (second[:blocks] + second[blocks:]))


def body(
    history, tile_blocks, tile_target, tile_source, tile_offset, delay_bins, incident, self_inv
):
    lag_rows = history.shape[0]
    tile_count, size = tile_blocks.shape[:2]
    slab_blocks = self_inv.shape[0]
    n_blk, n_lag = lax.axis_size("blk"), lax.axis_size("lag")
    all_blocks = delay_bins.shape[0]
    bits = n_blk.bit_length() - 1
    shift = all_blocks.bit_length() - 1
    slab_shift = slab_blocks.bit_length() - 1
    gather_bits = [1 << i for i in range(bits // 2)]
    exchange_bits = [1 << i for i in range(bits - 1, bits // 2 - 1, -1)]
    lag_shift = lag_rows.bit_length() - 1
    paired = n_lag == 2 and len(gather_bits) == 2
    cap = 2 * tile_count // n_blk
    n_pieces = 1 << len(gather_bits)
    plan = Plan(
        size,
        slab_shift,
        shift,
        lag_shift,
        n_pieces,
        cap,
        (3 if paired else n_pieces) * cap,
        tuple(gather_bits) if paired else (),
    )

    def hop(value, bit, other=None, flip=1):
        bits_of, flip = [bit, bit if other is None else other], flip if paired else 0
        pairs = [
            (j * n_lag + c, (j ^ bits_of[c % 2]) * n_lag + (c ^ flip))
            for j in range(n_blk)
            for c in range(n_lag)
        ]
        return lax.ppermute(value, ("blk", "lag"), pairs)

    if paired:
        first = hop(history[None], *gather_bits, flip=0)
    else:
        first = hop(history[None], gather_bits[0])
    ids = call(ids_kernel, "ids", pltpu.VMEM((min(all_blocks, 128), tile_count), jnp.int32), weight=8)
    code = call(
        lambda *refs: request_kernel(lag_rows * n_lag, shift, slab_shift, *refs),
        "request",
        pltpu.VMEM((1, 2 * tile_count), jnp.int32),
        ids,
        tile_source[None],
        tile_offset[None],
        delay_bins[None],
        weight=0,
    )

    def join(name, mine, other, weight, *extra):
        shape = (2 * mine.shape[0],) + mine.shape[1:]
        return call(
            lambda *refs: join_kernel(refs[0], refs[1], refs[-1]),
            name,
            pltpu.VMEM(shape, mine.dtype),
            mine,
            other,
            *extra,
            weight=weight,
        )

    own_code = code
    for bit in exchange_bits[:-1]:
        code = join("join", code, hop(code, bit), 8)
    far_code = hop(code, exchange_bits[-1])
    pieces, arrived = history[None], first
    for bit in gather_bits[1:]:
        pieces = join("gather", pieces, arrived, 0, tile_blocks)
        arrived = hop(pieces, bit, gather_bits[0]) if paired else hop(pieces, bit)

    n_hops = len(exchange_bits)

    n_slots = plan.slots << n_hops
    cuts = [0, n_slots // 64 * 16, max(n_slots // 2, n_slots * 7 // 12 // 16 * 16), n_slots]
    wide = -(-n_slots // 128) * 128
    scratch = [pltpu.SMEM((1, wide), jnp.int32), pltpu.SemaphoreType.DMA]

    def turned_tiles(run):
        return pltpu.VMEM(((cuts[run + 1] - cuts[run]) * size, size), tile_blocks.dtype)

    code, slot_tiles, columns, turned0 = call(
        lambda *refs: order_kernel(plan, n_hops, cuts[1], *refs),
        "order",
        (in_vmem(code), pltpu.VMEM((1, wide), jnp.int32), pltpu.VMEM((n_slots, size), jnp.int32), turned_tiles(0)),
        own_code,
        tile_target[None],
        code,
        tile_blocks,
        weight=0,
        scratch=scratch,
    )

    def select(name, groups, rows, weight, *after):
        return call(
            lambda *refs: select_kernel(plan, groups, *refs[len(after) :]),
            name,
            [pltpu.VMEM((n, size), jnp.bfloat16) for n in rows],
            *after,
            code,
            far_code,
            pieces,
            arrived,
            weight=weight,
        )

    def passes(i):
        return [d for d in range(1 << n_hops) if d >> i > 1 and (d >> i) & 1 and d % (1 << i) == 0]

    first_pass = passes(0) + [1]
    (send,) = select("select_send", [first_pass], [plan.slots * len(first_pass)], 16)
    rest = [d for d in range(2, 1 << n_hops) if d % 2 == 0]
    *picks, keep = select("select_keep", [[d] for d in rest + [0]], [plan.slots] * (len(rest) + 1), 16, send)
    held = dict(zip(rest, picks))
    keep, turned1 = call(
        lambda *refs: turn_kernel(cuts[1], cuts[2] - cuts[1], *refs),
        "turn",
        (in_vmem(keep), turned_tiles(1)),
        keep,
        slot_tiles,
        tile_blocks,
        weight=4,
        scratch=scratch,
    )
    landed = []
    for i, bit in enumerate(exchange_bits):
        onward, rows = passes(i), plan.slots << i
        if onward:
            if i:
                send = jnp.concatenate([held[d] for d in onward + [1 << i]], axis=0)
            passed = hop(send, bit)
            landed.append(passed[len(onward) * rows :])
        if i == n_hops - 1:
            inverse = pltpu.VMEM((slab_blocks * size, size), jnp.bfloat16)
            early, turned2, *inverses = call(
                lambda *refs: early_kernel(cuts, n_hops, *refs),
                "early",
                (pltpu.VMEM((slab_blocks, size), jnp.float32), turned_tiles(2), inverse, inverse),
                columns,
                slot_tiles,
                tile_blocks,
                self_inv,
                turned0,
                turned1,
                keep,
                *landed,
                weight=4,
                scratch=scratch,
            )
        if not onward:
            landed.append(hop(held[1 << i], bit))
        for k, d in enumerate(onward):
            here = d ^ (1 << i)
            held[here] = jnp.concatenate([held[here], passed[k * rows : (k + 1) * rows]], axis=0)
    mine = call(
        lambda *refs: couple_kernel(cuts, *refs),
        "couple",
        pltpu.VMEM((slab_blocks, size), jnp.float32),
        early,
        columns,
        turned1,
        turned2,
        landed[-1],
    )
    if n_lag == 2:
        other = lax.ppermute(mine, "lag", [(0, 1), (1, 0)])
    else:
        other = lax.psum(mine, "lag") - mine
    solved = call(
        solve_kernel,
        "solve",
        jax.ShapeDtypeStruct((slab_blocks, size), jnp.float32),
        mine,
        other,
        incident.reshape(slab_blocks, size),
        *inverses,
    )
    return solved.reshape(slab_blocks * size)


def solution(mesh):
    return jax.shard_map(
        body,
        mesh=mesh,
        in_specs=(
            P("lag", "blk"),
            P("blk", None, None),
            P("blk"),
            P("blk"),
            P("blk"),
            P(),
            P("blk"),
            P("blk", None, None),
        ),
        out_specs=P("blk"),
        check_vma=False,
    )
```

```python
import typing

import jax
import jax.numpy as jnp
from jax import lax
from jax.experimental import pallas as pl
from jax.experimental.pallas import tpu as pltpu
from jax.sharding import PartitionSpec as P


VMEM = pl.BlockSpec(memory_space=pltpu.VMEM)


class Plan(typing.NamedTuple):
    size: int
    slab_shift: int
    shift: int
    lag_shift: int
    pieces: int
    cap: int
    slots: int
    split: tuple


def call(kernel, name, outs, *operands, weight=0, scratch=()):
    return pl.pallas_call(
        kernel,
        out_shape=outs,
        in_specs=[VMEM] * len(operands),
        out_specs=jax.tree.map(lambda _: VMEM, outs),
        scratch_shapes=scratch,
        compiler_params=pltpu.CompilerParams(vmem_limit_bytes=16 * 1024 * 1024),
        cost_estimate=pl.CostEstimate(
            flops=weight << 32, bytes_accessed=weight << 24, transcendentals=0
        ),
        name=name,
    )(*(pltpu.with_memory_space_constraint(a, pltpu.VMEM) for a in operands))


def in_vmem(a):
    return pltpu.VMEM(a.shape, a.dtype)


def ids_kernel(out_ref):
    out_ref[...] = lax.broadcasted_iota(jnp.int32, out_ref.shape, 0)


def request_kernel(total_lags, shift, slab_shift, ids_ref, source_ref, offset_ref, delay_ref, code_ref):
    source = source_ref[...]
    chunk, lane = ids_ref.shape
    looked = jnp.zeros_like(source)
    for first in range(0, delay_ref.shape[1], chunk):
        delay = jnp.transpose(jnp.broadcast_to(delay_ref[:, first : first + chunk], (lane, chunk)))
        block = ids_ref[...] + first
        looked = looked + jnp.sum(jnp.where(block == source, delay, 0), axis=0, keepdims=True)
    lag = offset_ref[...] + looked
    lag = jnp.where(lag >= total_lags, lag - total_lags, lag)
    code_ref[:, :lane] = (lag << shift) | source
    owner = source >> slab_shift
    other = jnp.transpose(jnp.broadcast_to(owner, (lane, lane)))
    earlier = lax.broadcasted_iota(jnp.int32, (lane, lane), 0) < lax.broadcasted_iota(
        jnp.int32, (lane, lane), 1
    )
    alike = jnp.where((other == owner) & earlier, 1, 0)
    code_ref[:, lane:] = jnp.sum(alike, axis=0, keepdims=True)


def join_kernel(mine_ref, other_ref, out_ref):
    rows = mine_ref.shape[0]
    out_ref[:rows] = mine_ref[...]
    out_ref[rows:] = other_ref[...]


def ordinal(plan, piece, lag):
    if not plan.split:
        return jnp.where(piece < plan.pieces, piece, -1)
    low, high = plan.split
    turn = jnp.where(lag == 0, low, high)
    return jnp.where(
        piece == 0, 0, jnp.where(piece == turn, 1, jnp.where(piece == low + high, 2, -1))
    )


def select_kernel(plan, groups, near_ref, far_ref, near_pieces_ref, far_pieces_ref, *out_refs):
    size, cap, lag_shift = plan.size, plan.cap, plan.lag_shift
    blk, lag = lax.axis_index("blk"), lax.axis_index("lag")
    slabs = [r[q] for r in (near_pieces_ref, far_pieces_ref) for q in range(r.shape[0])]
    width = slabs[0].shape[1]
    table = [s[:, b : b + size] for s in slabs for b in range(0, width, size)]
    table = jnp.concatenate(
        [jnp.concatenate(table[: len(table) // 2]), jnp.concatenate(table[len(table) // 2 :])], axis=1
    )
    depth = table.shape[0]
    code = jnp.concatenate([near_ref[...], far_ref[...]], axis=0)
    tiles = code.shape[1] // 2
    address, place = code[:, :tiles], code[:, tiles:]
    source = address & ((1 << plan.shift) - 1)
    wanted = address >> plan.shift
    piece = (source >> plan.slab_shift) ^ blk
    half = wanted >> lag_shift
    if plan.split:
        low, high = plan.split
        same, turn = half == lag, jnp.where(lag == 0, low, high)
        slab = jnp.where((piece == 0) & same, 0, -1)
        slab = jnp.where(piece == turn, jnp.where(same, 1, 2), slab)
        slab = jnp.where((piece == low + high) & jnp.logical_not(same), 3, slab)
    else:
        slab = jnp.where((piece < plan.pieces) & (half == lag), piece, -1)
    inner = (source & ((1 << plan.slab_shift) - 1)) << lag_shift
    row = (slab << (plan.slab_shift + lag_shift)) + inner + (wanted & ((1 << lag_shift) - 1))
    row = jnp.where(slab >= 0, row, -1)
    rank = ordinal(plan, piece, lag)
    slot = jnp.where(rank >= 0, rank * cap + place, -1)

    def picked(chosen):
        lane = lax.broadcasted_iota(jnp.int32, chosen.shape, 1)
        low = chosen & (depth - 1)
        onehot = jnp.concatenate(
            [
                jnp.where(low == lane + first, 1.0, 0.0).astype(jnp.bfloat16)
                for first in range(0, depth, size)
            ],
            axis=1,
        )
        both = jnp.dot(onehot, table, preferred_element_type=jnp.float32)
        upper = chosen >> (depth.bit_length() - 1)
        rows = jnp.where(upper == 0, both[:, :size], jnp.where(upper == 1, both[:, size:], 0.0))
        return rows.astype(jnp.bfloat16)

    slot_id = lax.broadcasted_iota(jnp.int32, (plan.slots, tiles), 0)
    for group, out_ref in zip(groups, out_refs):
        for k, d in enumerate(group):
            there = jnp.where(slot_id == slot[d : d + 1], row[d : d + 1] + 1, 0)
            chosen = jnp.sum(there, axis=1, keepdims=True) - 1
            chosen = jnp.broadcast_to(chosen, (plan.slots, size))
            out_ref[k * plan.slots : (k + 1) * plan.slots, :] = picked(chosen)


def order_kernel(
    plan, hops, count, code_ref, target_ref, held_ref, tiles_ref, passed_ref, tile_ref, column_ref, turned_ref, *scratch
):
    tiles, size = tiles_ref.shape[:2]
    passed_ref[...] = held_ref[...]
    blk, lag = lax.axis_index("blk"), lax.axis_index("lag")
    source = code_ref[:, :tiles] & ((1 << plan.shift) - 1)
    place = code_ref[:, tiles:]
    apart = (source >> plan.slab_shift) ^ blk
    piece, high = apart & (plan.pieces - 1), apart >> (plan.pieces.bit_length() - 1)
    plane = sum(((high >> (hops - 1 - i)) & 1) << i for i in range(hops))
    sender = jnp.zeros_like(plane) + lag
    if plan.split:
        for i in range(hops):
            sender = sender ^ ((plane >> i) & 1)
    rank = ordinal(plan, piece, sender)
    slot = jnp.where(rank >= 0, plane * plan.slots + rank * plan.cap + place, -1)
    wide = tile_ref.shape[1]
    slot = jnp.transpose(jnp.broadcast_to(slot, (wide, tiles)))
    target = jnp.transpose(jnp.broadcast_to(target_ref[...], (wide, tiles)))
    here = slot == lax.broadcasted_iota(jnp.int32, (tiles, wide), 1)
    tile = jnp.where(here, lax.broadcasted_iota(jnp.int32, (tiles, wide), 0), 0)
    tile_ref[...] = jnp.minimum(jnp.sum(tile, axis=0, keepdims=True), tiles - 1)
    target = jnp.sum(jnp.where(here, target + 1, 0), axis=0, keepdims=True) - 1
    column_ref[...] = jnp.transpose(jnp.broadcast_to(target, (size, wide)))[: column_ref.shape[0], :]
    turn(0, count, tile_ref, tiles_ref, turned_ref, *scratch)


def turn(first, count, tile_ref, tiles_ref, turned_ref, index, sem):
    copy = pltpu.make_async_copy(tile_ref, index, sem)
    copy.start()
    copy.wait()
    size = tiles_ref.shape[1]
    for s in range(count):
        turned_ref[s * size : (s + 1) * size, :] = jnp.transpose(tiles_ref[index[0, first + s]])


def turn_kernel(first, count, held_ref, tile_ref, tiles_ref, passed_ref, turned_ref, *scratch):
    passed_ref[...] = held_ref[...]
    turn(first, count, tile_ref, tiles_ref, turned_ref, *scratch)


def products(first, column_ref, row_refs, turned_refs, blocks):
    rows = jnp.concatenate([r[...] for r in row_refs], axis=0).astype(jnp.float32)
    count, size = rows.shape
    target = column_ref[first : first + count, :]
    left = jnp.stack([jnp.where(target == b, rows, 0.0) for b in range(blocks)], axis=0)
    left = left.astype(jnp.bfloat16)
    total = jnp.zeros((blocks, size), jnp.float32)
    for turned_ref, start, held in turned_refs:
        low, high = max(first, start), min(first + count, start + held)
        if low < high:
            part = left[:, low - first : high - first].reshape(blocks, (high - low) * size)
            total = total + jnp.dot(
                part,
                turned_ref[(low - start) * size : (high - start) * size, :],
                preferred_element_type=jnp.float32,
            )
    return total


def early_kernel(
    cuts, n_rows, column_ref, tile_ref, tiles_ref, inverse_ref, turned0_ref, turned1_ref, *refs
):
    row_refs, (sum_ref, turned_ref, high_ref, low_ref, index, sem) = refs[:n_rows], refs[n_rows:]
    turned = [(turned0_ref, cuts[0], cuts[1] - cuts[0]), (turned1_ref, cuts[1], cuts[2] - cuts[1])]
    sum_ref[...] = products(0, column_ref, row_refs, turned, sum_ref.shape[0])
    turn(cuts[2], cuts[3] - cuts[2], tile_ref, tiles_ref, turned_ref, index, sem)
    blocks, size = inverse_ref.shape[:2]
    for b in range(blocks):
        whole = jnp.transpose(inverse_ref[b])
        high = whole.astype(jnp.bfloat16)
        high_ref[b * size : (b + 1) * size, :] = high
        low = whole - high.astype(jnp.float32)
        low_ref[b * size : (b + 1) * size, :] = low.astype(jnp.bfloat16)


def couple_kernel(cuts, early_ref, column_ref, turned1_ref, turned2_ref, rows_ref, out_ref):
    turned = [(turned1_ref, cuts[1], cuts[2] - cuts[1]), (turned2_ref, cuts[2], cuts[3] - cuts[2])]
    first = cuts[3] - rows_ref.shape[0]
    out_ref[...] = early_ref[...] + products(first, column_ref, [rows_ref], turned, out_ref.shape[0])


def solve_kernel(mine_ref, other_ref, incident_ref, high_ref, low_ref, out_ref):
    blocks, size = incident_ref.shape
    excite = incident_ref[...] - (mine_ref[...] + other_ref[...])
    high = excite.astype(jnp.bfloat16).astype(jnp.float32)
    block_id = lax.broadcasted_iota(jnp.int32, (blocks, size), 0)

    def spread(rows):
        parts = [jnp.where(block_id == b, rows, 0.0) for b in range(blocks)]
        return jnp.concatenate(parts, axis=1)

    left = jnp.concatenate([spread(high), spread(excite - high)], axis=0).astype(jnp.bfloat16)
    first = jnp.dot(left, high_ref[...], preferred_element_type=jnp.float32)
    second = jnp.dot(left, low_ref[...], preferred_element_type=jnp.float32)
    out_ref[...] = first[:blocks] + (first[blocks:] + (second[:blocks] + second[blocks:]))


def body(
    history, tile_blocks, tile_target, tile_source, tile_offset, delay_bins, incident, self_inv
):
    lag_rows = history.shape[0]
    tile_count, size = tile_blocks.shape[:2]
    slab_blocks = self_inv.shape[0]
    n_blk, n_lag = lax.axis_size("blk"), lax.axis_size("lag")
    all_blocks = delay_bins.shape[0]
    bits = n_blk.bit_length() - 1
    shift = all_blocks.bit_length() - 1
    slab_shift = slab_blocks.bit_length() - 1
    gather_bits = [1 << i for i in range(bits // 2)]
    exchange_bits = [1 << i for i in range(bits - 1, bits // 2 - 1, -1)]
    lag_shift = lag_rows.bit_length() - 1
    paired = n_lag == 2 and len(gather_bits) == 2
    cap = 2 * tile_count // n_blk
    n_pieces = 1 << len(gather_bits)
    plan = Plan(
        size,
        slab_shift,
        shift,
        lag_shift,
        n_pieces,
        cap,
        (3 if paired else n_pieces) * cap,
        tuple(gather_bits) if paired else (),
    )

    def hop(value, bit, other=None, flip=1):
        bits_of, flip = [bit, bit if other is None else other], flip if paired else 0
        pairs = [
            (j * n_lag + c, (j ^ bits_of[c % 2]) * n_lag + (c ^ flip))
            for j in range(n_blk)
            for c in range(n_lag)
        ]
        return lax.ppermute(value, ("blk", "lag"), pairs)

    if paired:
        first = hop(history[None], *gather_bits, flip=0)
    else:
        first = hop(history[None], gather_bits[0])
    ids = call(ids_kernel, "ids", pltpu.VMEM((min(all_blocks, 128), tile_count), jnp.int32), weight=8)
    code = call(
        lambda *refs: request_kernel(lag_rows * n_lag, shift, slab_shift, *refs),
        "request",
        pltpu.VMEM((1, 2 * tile_count), jnp.int32),
        ids,
        tile_source[None],
        tile_offset[None],
        delay_bins[None],
        weight=0,
    )

    def join(name, mine, other, weight, *extra):
        shape = (2 * mine.shape[0],) + mine.shape[1:]
        return call(
            lambda *refs: join_kernel(refs[0], refs[1], refs[-1]),
            name,
            pltpu.VMEM(shape, mine.dtype),
            mine,
            other,
            *extra,
            weight=weight,
        )

    own_code = code
    for bit in exchange_bits[:-1]:
        code = join("join", code, hop(code, bit), 8)
    far_code = hop(code, exchange_bits[-1])
    pieces, arrived = history[None], first
    for bit in gather_bits[1:]:
        pieces = join("gather", pieces, arrived, 0, tile_blocks)
        arrived = hop(pieces, bit, gather_bits[0]) if paired else hop(pieces, bit)

    n_hops = len(exchange_bits)

    n_slots = plan.slots << n_hops
    cuts = [0, n_slots // 48 * 16, max(n_slots // 2, n_slots * 2 // 3 // 16 * 16), n_slots]
    wide = -(-n_slots // 128) * 128
    scratch = [pltpu.SMEM((1, wide), jnp.int32), pltpu.SemaphoreType.DMA]

    def turned_tiles(run):
        return pltpu.VMEM(((cuts[run + 1] - cuts[run]) * size, size), tile_blocks.dtype)

    code, slot_tiles, columns, turned0 = call(
        lambda *refs: order_kernel(plan, n_hops, cuts[1], *refs),
        "order",
        (in_vmem(code), pltpu.VMEM((1, wide), jnp.int32), pltpu.VMEM((n_slots, size), jnp.int32), turned_tiles(0)),
        own_code,
        tile_target[None],
        code,
        tile_blocks,
        weight=0,
        scratch=scratch,
    )

    def select(name, groups, rows, weight, *after):
        return call(
            lambda *refs: select_kernel(plan, groups, *refs[len(after) :]),
            name,
            [pltpu.VMEM((n, size), jnp.bfloat16) for n in rows],
            *after,
            code,
            far_code,
            pieces,
            arrived,
            weight=weight,
        )

    def passes(i):
        return [d for d in range(1 << n_hops) if d >> i > 1 and (d >> i) & 1 and d % (1 << i) == 0]

    first_pass = passes(0) + [1]
    (send,) = select("select_send", [first_pass], [plan.slots * len(first_pass)], 16)
    rest = [d for d in range(2, 1 << n_hops) if d % 2 == 0]
    *picks, keep = select("select_keep", [[d] for d in rest + [0]], [plan.slots] * (len(rest) + 1), 16, send)
    held = dict(zip(rest, picks))
    keep, turned1 = call(
        lambda *refs: turn_kernel(cuts[1], cuts[2] - cuts[1], *refs),
        "turn",
        (in_vmem(keep), turned_tiles(1)),
        keep,
        slot_tiles,
        tile_blocks,
        weight=4,
        scratch=scratch,
    )
    landed = []
    for i, bit in enumerate(exchange_bits):
        onward, rows = passes(i), plan.slots << i
        if onward:
            if i:
                send = jnp.concatenate([held[d] for d in onward + [1 << i]], axis=0)
            passed = hop(send, bit)
            landed.append(passed[len(onward) * rows :])
        if i == n_hops - 1:
            inverse = pltpu.VMEM((slab_blocks * size, size), jnp.bfloat16)
            early, turned2, *inverses = call(
                lambda *refs: early_kernel(cuts, n_hops, *refs),
                "early",
                (pltpu.VMEM((slab_blocks, size), jnp.float32), turned_tiles(2), inverse, inverse),
                columns,
                slot_tiles,
                tile_blocks,
                self_inv,
                turned0,
                turned1,
                keep,
                *landed,
                weight=4,
                scratch=scratch,
            )
        if not onward:
            landed.append(hop(held[1 << i], bit))
        for k, d in enumerate(onward):
            here = d ^ (1 << i)
            held[here] = jnp.concatenate([held[here], passed[k * rows : (k + 1) * rows]], axis=0)
    mine = call(
        lambda *refs: couple_kernel(cuts, *refs),
        "couple",
        pltpu.VMEM((slab_blocks, size), jnp.float32),
        early,
        columns,
        turned1,
        turned2,
        landed[-1],
    )
    if n_lag == 2:
        other = lax.ppermute(mine, "lag", [(0, 1), (1, 0)])
    else:
        other = lax.psum(mine, "lag") - mine
    solved = call(
        solve_kernel,
        "solve",
        jax.ShapeDtypeStruct((slab_blocks, size), jnp.float32),
        mine,
        other,
        incident.reshape(slab_blocks, size),
        *inverses,
    )
    return solved.reshape(slab_blocks * size)


def solution(mesh):
    return jax.shard_map(
        body,
        mesh=mesh,
        in_specs=(
            P("lag", "blk"),
            P("blk", None, None),
            P("blk"),
            P("blk"),
            P("blk"),
            P(),
            P("blk"),
            P("blk", None, None),
        ),
        out_specs=P("blk"),
        check_vma=False,
    )
```
